32 devices in a mesh: dp: 4 (over y, core), ty: 4 (over z), tx: 2 (over x).
Axes of the slice: x: 2, y: 2, z: 4, core: 2. Of those that a mesh axis runs over, the one named last changes fastest.
Arguments:
- features: bfloat16 [4, 256, 128, 128], P('dp', 'ty', 'tx'), may hold values from -6 to 6
- filter_one: bfloat16 [3, 3, 128, 128], P(None, None, None, 'dp'), may hold values from -0.1875 to 0.1875
- filter_two: bfloat16 [3, 3, 128, 128], P(None, None, None, 'dp'), may hold values from -0.1875 to 0.1875
- speedup: float32 [4, 256, 128], P('dp', 'ty', 'tx'), may hold values from 0.5 to 2
- land_mask: int32 [4, 256, 128], P('dp', 'ty', 'tx'), may hold values 0 or 1
- offsets: int32 [4, 2], P('dp'), may hold values from 0 to 1023
- upstream: bfloat16 [4, 256, 128, 128], P('dp', 'ty', 'tx'), may hold values from -6 to 6
Outputs:
- output: bfloat16 [4, 256, 128, 128], P('dp', 'ty', 'tx')
- grad_input: bfloat16 [4, 256, 128, 128], P('dp', 'ty', 'tx')
- grad_one: float32 [3, 3, 128, 128], P(None, None, None, 'dp')
- grad_two: float32 [3, 3, 128, 128], P(None, None, None, 'dp')
The draws below stay inside these ranges and needn't reach their ends.
All inputs are finite; a program needn't handle non-finite values. No bound on the sum of `land_mask` on one device may be relied on, other than what follows from the above.
Results may differ from the reference program's by a relative error of at most 0.014.
Values may be sent and summed in bfloat16 or wider, within the bound.
No kernel may reach another device: no remote copies, remote signals or barrier semaphores. Data moves between devices by JAX's collectives and lax.ppermute only.
A program may use at most 64 MiB of HBM per device.

```python
import math
import jax
import jax.numpy as jnp
from jax import lax

C = 128
BATCH = 4
CROP_H = 256
CROP_W = 128


def place_ends(result, key, smallest, largest):
    longest = result.shape.index(max(result.shape))
    spots = []
    for shift in (0, 1):
        where = [jax.random.randint(jax.random.fold_in(key, axis), (), 0, length) for axis, length in enumerate(result.shape)]
        where[longest] = (where[longest] + shift) % result.shape[longest]
        spots.append(tuple(where))
    return result.at[spots[0]].set(smallest).at[spots[1]].set(largest)


def with_spikes(values, rng, source, target, shards_of, factor):
    owner, partner = [(jnp.arange(values.shape[position]) // (values.shape[position] // shards_of)).reshape([-1 if axis == position else 1 for axis in range(values.ndim)]) for position in (source, target)]
    chosen = jax.random.permutation(rng, shards_of)[partner]
    strong = (owner == chosen) | (owner == (partner + shards_of // 2) % shards_of)
    return jnp.where(strong, factor * values, values)


def steps_of(stream_key, dims, cuts, low, high):
    loudness, own = 1.0, jax.random.fold_in(stream_key, 6)
    for axis_at, parts in cuts:
        draws = jnp.exp(jax.random.uniform(jax.random.fold_in(own, axis_at), (parts,), jnp.float32, low / len(cuts), high / len(cuts)))
        loudness = loudness * jnp.repeat(draws, dims[axis_at] // parts).reshape([-1 if axis == axis_at else 1 for axis in range(len(dims))])
    return loudness


def gaussian(own_key, shape, deviation, most, cuts=(), kind=jnp.bfloat16):
    values = jax.random.normal(own_key, shape, jnp.float32) * deviation
    if len(cuts) > 0:
        values = steps_of(own_key, shape, cuts, -0.22, 0.18) * values
    return jnp.clip(values, min=-most, max=most).astype(kind)


def heavy_noise(rng, shape, deviation, most, split, heavy, kind=jnp.bfloat16):
    values = deviation * jax.random.normal(rng, shape, jnp.float32)
    if split:
        values = values * steps_of(rng, shape, split, -0.22, 0.18)
    return jnp.clip(with_spikes(values, jax.random.fold_in(rng, 3), *heavy), -most, most).astype(kind)


def setup_inputs(seed: int = 0) -> dict:
    streams_of = jax.random.split(jax.random.key(seed), 8)
    return {
        "features": gaussian(streams_of[0], (BATCH, CROP_H, CROP_W, C), 1.0, 6.0, ((0, 4), (1, 4), (2, 2))),
        "filter_one": gaussian(streams_of[1], (3, 3, C, C), (9 * C) ** -0.5, 0.1875, ((3, 4),)),
        "filter_two": gaussian(streams_of[2], (3, 3, C, C), (9 * C) ** -0.5, 0.1875, ((3, 4),)),
        "speedup": jnp.clip(jnp.exp(math.log(2.0) - 1.3862944 * jax.random.uniform(streams_of[3], (BATCH, CROP_H, CROP_W), jnp.float32) ** steps_of(streams_of[3], (BATCH, CROP_H, CROP_W), ((0, 4), (1, 4), (2, 2)), -0.2, 0.2)), 0.5, 2.0),
        "land_mask": place_ends((jax.random.randint(streams_of[4], (BATCH, CROP_H, CROP_W), 0, 2) < 1).astype(jnp.int32), jax.random.fold_in(streams_of[4], 1), 0, 1),
        "offsets": place_ends(jax.random.randint(streams_of[5], (BATCH, 2), 0, 1024), jax.random.fold_in(streams_of[5], 1), 0, 1023).astype(jnp.int32),
        "upstream": heavy_noise(streams_of[6], (BATCH, CROP_H, CROP_W, C), 1.0, 6.0, ((0, 4), (1, 4), (2, 2)), (0, 3, 4, 2.0)),
    }


def conv_same(values, kernel):
    return lax.conv_general_dilated(values, kernel, (1, 1), ((1, 1), (1, 1)), dimension_numbers=('NHWC', 'HWIO', 'NHWC'), preferred_element_type=jnp.float32)

def flipped(kernel):
    return jnp.flip(kernel, (0, 1)).transpose(0, 1, 3, 2)

def filter_grad(values, grads):
    padded = jnp.pad(values, ((0, 0), (1, 1), (1, 1), (0, 0))).astype(jnp.float32)
    grads32 = grads.astype(jnp.float32)
    height = grads.shape[1]
    breadth = grads.shape[2]
    result_rows = []
    for row_tap in range(3):
        taps_row = []
        for col_tap in range(3):
            window = padded[:, row_tap:row_tap + height, col_tap:col_tap + breadth, :]
            taps_row.append(jnp.einsum('bhwc,bhwd->cd', window, grads32))
        result_rows.append(jnp.stack(taps_row))
    return jnp.stack(result_rows)

def reference(features, filter_one, filter_two, speedup, land_mask, offsets, upstream):
    row_pos = (offsets[:, 0:1] + jnp.arange(CROP_H, dtype=jnp.int32)[None, :]).astype(jnp.float32)
    col_pos = (offsets[:, 1:2] + jnp.arange(CROP_W, dtype=jnp.int32)[None, :]).astype(jnp.float32)
    factor = jnp.where(land_mask == 1, speedup, jnp.float32(1.0))
    factor = factor / (1.0 + row_pos / 512.0)[:, :, None] / (1.0 + col_pos / 1024.0)[:, None, :]
    pre_one = conv_same(features, filter_one)
    sigmoid_one = jax.nn.sigmoid(pre_one)
    hidden = (pre_one * sigmoid_one * factor[..., None]).astype(jnp.bfloat16)
    output = conv_same(hidden, filter_two).astype(jnp.bfloat16)
    grad_hidden = conv_same(upstream, flipped(filter_two))
    grad_pre = (grad_hidden * factor[..., None] * sigmoid_one * (1.0 + pre_one * (1.0 - sigmoid_one))).astype(jnp.bfloat16)
    grad_input = conv_same(grad_pre, flipped(filter_one)).astype(jnp.bfloat16)
    grad_scale = 1.0 / jnp.sqrt(jnp.float32(BATCH * CROP_H * CROP_W))
    grad_two = filter_grad(hidden, upstream) * grad_scale
    grad_one = filter_grad(features, grad_pre) * grad_scale
    return (output, grad_input, grad_one, grad_two)
```

```python
import functools
import math

import jax
import jax.numpy as jnp
from jax import lax
from jax.experimental import pallas as pl
from jax.experimental.pallas import tpu as pltpu
from jax.sharding import PartitionSpec as P

F32 = jnp.float32
BF16 = jnp.bfloat16
RIM = 16
PAST = 8
CHUNK = 16
PLANES = 5
VMEM = pl.BlockSpec(memory_space=pltpu.VMEM)
HBM = pl.BlockSpec(memory_space=pltpu.HBM)
MIB = 1024 * 1024
SMALL = pltpu.CompilerParams(vmem_limit_bytes=8 * MIB)
MEDIUM = pltpu.CompilerParams(vmem_limit_bytes=16 * MIB)


def in_hbm(*arrays):
    return [pltpu.with_memory_space_constraint(array, pltpu.HBM) for array in arrays]


def is_odd(axis):
    return lax.rem(lax.axis_index(axis), 2) == 1


def kind_pairs(count, kind):
    return [(i, i + 1) for i in range(kind, count - 1, 2)]


def swaps(axis, sent):
    got = []
    for kind in reversed(range(len(sent))):
        pairs = [p for i, j in kind_pairs(lax.axis_size(axis), kind) for p in ((i, j), (j, i))]
        got.append(lax.ppermute(sent[kind], axis, pairs))
    return got[::-1]


def sides(axis, got):
    odd = is_odd(axis)
    first = got[0]
    second = got[1] if len(got) > 1 else jnp.zeros_like(first)
    return jnp.where(odd, first, second), jnp.where(odd, second, first)


def rim_of(before, after):
    channels = after[0].shape[1]
    at = lax.broadcasted_iota(jnp.int32, (RIM, channels), 0)
    rim = jnp.where(at == 0, after[0], 0.0)
    if after[1] is not None:
        rim = jnp.where(at == 1, after[1], rim)
    if before[0] is not None:
        rim = jnp.where(at == RIM - 2, before[0], rim)
    return jnp.where(at == RIM - 1, before[1], rim)


def factor_tile(line, channels):
    high = line.astype(BF16).astype(F32)
    low = (line - high).astype(BF16).astype(F32)
    line = jnp.concatenate([high, low, jnp.zeros((RIM - 2, line.shape[1]), F32)])
    past = channels - line.shape[1]
    return line if past == 0 else jnp.concatenate([line, jnp.zeros((RIM, past), F32)], axis=1)


def tx_sides(got, height):
    result = []
    for rows in sides("tx", [ref[...].astype(F32) for ref in got]):
        lines = [rows[n * height : (n + 1) * height] for n in range(4)]
        parts = jnp.transpose(rows[4 * height :])
        result.append((lines, parts[:height, 0:1] + parts[:height, 1:2]))
    return result


def two_parts(column, channels):
    high = column.astype(BF16).astype(F32)
    low = (column - high).astype(BF16).astype(F32)
    lane = lax.broadcasted_iota(jnp.int32, (column.shape[0], channels), 1)
    return jnp.where(lane == 0, high, jnp.where(lane == 1, low, 0.0))


def columns_kernel(kinds_tx, offsets, features, upstream, speedup, land, one, two, *rest):
    sent, rest = rest[:kinds_tx], rest[kinds_tx:]
    factor_ref, filters_ref, own_columns, spread, blocks, speed, mask, place, sems = rest
    _, height, breadth = speedup.shape
    channels = features.shape[3]
    taps = one.shape[0]
    ends = (pl.ds(0, RIM), pl.ds(breadth - RIM, RIM))
    moves = [(speedup, speed), (land, mask), (offsets, place)]
    moves += [
        (ref.at[0, :, ends[side], :], blocks.at[2 * array + side])
        for array, ref in enumerate((features, upstream))
        for side in range(2)
    ]
    moves += [(one, filters_ref.at[pl.ds(0, taps)]), (two, filters_ref.at[pl.ds(taps, taps)])]
    copies = [pltpu.make_async_copy(*move, sems.at[n]) for n, move in enumerate(moves)]
    for copy in copies:
        copy.start()
    for copy in copies[:3]:
        copy.wait()
    shape = (height, breadth)
    row = place[0, 0] + lax.axis_index("ty") * height + lax.broadcasted_iota(jnp.int32, shape, 0)
    col = place[0, 1] + lax.axis_index("tx") * breadth + lax.broadcasted_iota(jnp.int32, shape, 1)
    factor = jnp.where(mask[0] == 1, speed[0], jnp.float32(1.0))
    factor = factor / (1.0 + row.astype(F32) / 512.0) / (1.0 + col.astype(F32) / 1024.0)
    factor_ref[...] = factor
    odd = is_odd("tx")

    def column(at):
        return spread[pl.ds(at, height, stride=RIM), :]

    heads, tails = [], []
    for array in range(2):
        copies[3 + 2 * array].wait()
        spread[...] = blocks[2 * array].astype(F32).reshape(height * RIM, channels)
        heads += [column(0), column(1)]
        copies[4 + 2 * array].wait()
        spread[...] = blocks[2 * array + 1].astype(F32).reshape(height * RIM, channels)
        tails += [column(RIM - 2), column(RIM - 1)]
    across = jnp.transpose(factor)
    heads.append(factor_tile(across[:1], channels))
    tails.append(factor_tile(across[breadth - 1 :], channels))
    for plane in range(PLANES):
        rows = slice(plane * height, min((plane + 1) * height, sent[0].shape[0]))
        sent[0][rows] = jnp.where(odd, heads[plane], tails[plane]).astype(BF16)
        if kinds_tx == 2:
            sent[1][rows] = jnp.where(odd, tails[plane], heads[plane]).astype(BF16)
    for array in range(2):
        own_columns[2 * array] = heads[2 * array].astype(BF16)
        own_columns[2 * array + 1] = tails[2 * array + 1].astype(BF16)
    for copy in copies[7:]:
        copy.wait()


def rows_kernel(kinds_tx, edges, factor_ref, *rest):
    got, sent = rest[:kinds_tx], rest[kinds_tx:]
    height, breadth = factor_ref.shape
    channels = edges.shape[3]
    across = jnp.transpose(factor_ref[...])
    (before, factor_before), (after, factor_after) = tx_sides(got, height)

    def message(side, lines, edge):
        planes = []
        for array in range(2):
            for n, line in enumerate(lines):
                rim = rim_of(
                    [before[2 * array + i][line : line + 1] for i in range(2)],
                    [after[2 * array + i][line : line + 1] for i in range(2)],
                )
                planes.append(jnp.concatenate([edges[2 * array + side, n].astype(F32), rim]))
        own = two_parts(across[:, edge : edge + 1], channels)
        rim = rim_of(
            (None, two_parts(factor_before[edge : edge + 1], channels)),
            (two_parts(factor_after[edge : edge + 1], channels), None),
        )
        planes.append(jnp.concatenate([own, rim]))
        return planes

    heads = message(0, (0, 1), 0)
    tails = message(1, (height - 2, height - 1), height - 1)
    odd = is_odd("ty")
    for plane in range(PLANES):
        sent[0][plane] = jnp.where(odd, heads[plane], tails[plane]).astype(BF16)
        if len(sent) == 2:
            sent[1][plane] = jnp.where(odd, tails[plane], heads[plane]).astype(BF16)


def pair_weights(target, block_of):
    channels = target.shape[2] // 2
    for half in range(2):
        for s in range(2):
            for t in range(2):
                a = 2 * half + s - t
                for e in range(3):
                    block = block_of(a, e) if 0 <= a <= 2 else jnp.zeros((channels, channels), BF16)
                    at = (3 * s + e) * channels
                    target[half, at : at + channels, t * channels : (t + 1) * channels] = block


def store_taps(target, where, s, wide, width):
    channels = wide.shape[-1]
    axis = wide.ndim - 2
    for e in range(3):
        if e == 1:
            moved = wide
        else:
            moved = pltpu.roll(wide, 1 if e == 0 else wide.shape[axis] - 1, axis)
        moved = moved[..., :width, :].astype(BF16)
        target[where, :, (3 * s + e) * channels : (3 * s + e + 1) * channels] = moved


def pair_conv(source, weights, at, pairs):
    _, width, depth = source.shape
    upper = source[at : at + pairs].reshape(pairs * width, depth)
    lower = source[at + 1 : at + 1 + pairs].reshape(pairs * width, depth)
    return deep_product(upper, lower, weights)


def deep_product(upper, lower, weights):
    _, depth, lanes = weights.shape
    return jnp.dot(
        jnp.concatenate([upper, lower], axis=1),
        weights[...].reshape(2 * depth, lanes),
        preferred_element_type=F32,
    )


def outer(grads, source):
    return lax.dot_general(grads, source, (((0,), (0,)), ((), ())), preferred_element_type=F32)


def own_kernel(
    features, upstream, factor_ref, x6, u6, up2, factors, edge_factors, edges, cells, sems
):
    _, height, breadth, channels = features.shape
    arrays = (features, upstream)
    parts = sems.shape[1]
    rows = height // parts
    copies = [
        [
            pltpu.make_async_copy(
                ref.at[0, pl.ds(n * rows, rows)],
                cells.at[array, pl.ds(n * rows, rows)],
                sems.at[array, n],
            )
            for array, ref in enumerate(arrays)
        ]
        for n in range(parts)
    ]
    for pair in copies:
        for copy in pair:
            copy.start()
    across = jnp.transpose(factor_ref[...])
    for i in range(height):
        line = jnp.broadcast_to(across[:, i : i + 1], (breadth, channels))
        if i in (0, height - 1):
            edge_factors[min(i, 1)] = line
        else:
            factors[(i - 1) // 2, (i - 1) % 2] = line

    def spread(q, carry):
        for s in range(2):
            for array, target in enumerate((x6, u6)):
                line = cells[array, 2 * q + s]
                store_taps(target, q, s, line.astype(F32), breadth)
            up2[q, :, s * channels : (s + 1) * channels] = line
        return carry

    for n, pair in enumerate(copies):
        for copy in pair:
            copy.wait()
        lax.fori_loop(n * rows // 2, (n + 1) * rows // 2, spread, 0)
    for array in range(2):
        edges[2 * array] = cells[array, :2]
        edges[2 * array + 1] = cells[array, height - 2 :]


def activations(pre, grad, factor):
    s = 0.5 * jnp.tanh(0.5 * pre) + 0.5
    fs = factor * s
    return pre * fs, grad * fs * (1.0 + pre * (1.0 - s))


class Beside:
    def __init__(self, array, got_tx, own_columns, columns):
        channels = columns.shape[2]
        height = columns.shape[1] - PAST
        self.array, self.columns, self.count = array, columns, height // 2
        (before, factor_before), (after, factor_after) = tx_sides(got_tx, height)
        own = own_columns[...].astype(F32)
        lines = (
            before[2 * array],
            before[2 * array + 1],
            own[2 * array],
            own[2 * array + 1],
            after[2 * array],
            after[2 * array + 1],
            jnp.broadcast_to(factor_before, (height, channels)),
            jnp.broadcast_to(factor_after, (height, channels)),
        )
        for n, line in enumerate(lines):
            columns[n, :height] = line
        columns[:, height:] = jnp.zeros((len(lines), PAST, channels), F32)

    def rows(self, n, begin):
        return self.columns[n, pl.ds(begin, self.count, stride=2), :]

    def conv(self, taps6, weights):
        count, channels = self.count, self.columns.shape[2]
        for half in range(2):
            for s in range(2):
                for side in range(2):
                    for e in range(3):
                        at = (3 * s + e) * channels
                        taps6[half, side * count : (side + 1) * count, at : at + channels] = (
                            self.rows(3 * side + e, 2 * half + s).astype(BF16)
                        )
        return deep_product(taps6[0], taps6[1], weights)

    def factor(self, t):
        return jnp.concatenate([self.rows(6, 1 + t), self.rows(7, 1 + t)])


def rims_of(lines, begin, pairs, count):
    return [
        [
            rim_of((None, lines[t, m : m + 1, :]), (lines[t, count + m : count + m + 1, :], None))
            for t in range(2)
        ]
        for m in range(begin, begin + pairs)
    ]


def middle_kernel(kinds_tx, n_dp, x6_in, u6_in, own_columns, factors, *rest):
    got_tx, rest = rest[:kinds_tx], rest[kinds_tx:]
    shards, rest = rest[:n_dp], rest[n_dp:]
    x6, u6, h6, gp2, filters_ref, w_one, w_up, beside_pre = rest[:8]
    columns, beside6, beside_hidden, hidden_rims, edge_cells = rest[8:13]
    pres, grads = rest[13:15], rest[15:17]
    count, breadth, _ = x6.shape
    channels = columns.shape[2]
    mine = shards[0].shape[1]
    me = lax.axis_index("dp")
    for partner, shard in enumerate(shards):
        slot = jnp.bitwise_xor(me, partner)
        filters_ref[:, pl.ds(pl.multiple_of(slot * mine, mine), mine), :] = shard[...]
    pair_weights(w_one, lambda a, e: jnp.transpose(filters_ref[3 * a + e]))
    (before, _), (after, _) = tx_sides(got_tx, 2 * count)
    for array in range(2):
        edge_cells[2 * array] = before[2 * array + 1]
        edge_cells[2 * array + 1] = after[2 * array]
    spot = lax.broadcasted_iota(jnp.int32, (RIM, channels), 0)
    first, last = slice(0, RIM), slice(breadth - RIM, breadth)

    def patch(array, begin, end):
        source, target = ((x6_in, x6), (u6_in, u6))[array]
        for q in range(begin, end):
            for s in range(2):
                i = 2 * q + s
                for e, rows, at in ((0, first, 0), (2, last, RIM - 1)):
                    cell = edge_cells[2 * array + e // 2, i : i + 1, :]
                    lanes = slice((3 * s + e) * channels, (3 * s + e + 1) * channels)
                    value = jnp.where(spot == at, cell, source[q, rows, lanes].astype(F32))
                    target[q, rows, lanes] = value.astype(BF16)

    def convolve(n, at, pairs):
        rows = pairs * breadth
        pres[n % 2][:rows] = pair_conv(x6, w_one, at, pairs)
        grads[n % 2][:rows] = pair_conv(u6, w_up, at, pairs)

    def activate(n, at, pairs):
        rows = pairs * breadth
        here = slice(at, at + pairs)
        for t in range(2):
            lanes = slice(t * channels, (t + 1) * channels)
            hidden, grad_pre = activations(
                pres[n % 2][:rows, lanes],
                grads[n % 2][:rows, lanes],
                factors[here, t].reshape(rows, channels),
            )
            hidden = hidden.reshape(pairs, breadth, channels)
            grad_pre = grad_pre.astype(BF16).reshape(pairs, breadth, channels)
            store_taps(
                h6, here, t, jnp.concatenate([hidden, hidden_rims[here, t]], axis=1), breadth
            )
            gp2[at + t : at + t + pairs, :, (1 - t) * channels : (2 - t) * channels] = grad_pre

    chunks = [(0, 0)]
    while sum(chunks[-1]) < count - 1:
        left = count - 1 - sum(chunks[-1])
        chunks.append((sum(chunks[-1]), min(left, CHUNK, max(3, (left + 1) // 2))))
    del chunks[0]
    done = 0
    for n, (at, pairs) in enumerate(chunks):
        for array in range(2):
            patch(array, done, at + pairs + 1)
        done = at + pairs + 1
        if n == 0:
            pair_weights(w_up, lambda a, e: filters_ref[9 + 3 * (2 - a) + (2 - e)])
        convolve(n, at, pairs)
        if n == 0:
            beside = Beside(0, got_tx, own_columns, columns)
            beside_pre[...] = beside.conv(beside6, w_one)
            for t in range(2):
                lanes = slice(t * channels, (t + 1) * channels)
                beside_hidden[t], _ = activations(beside_pre[:, lanes], 0.0, beside.factor(t))
        for m, rims in enumerate(rims_of(beside_hidden, at, pairs, count)):
            for t in range(2):
                hidden_rims[at + m, t] = rims[t]
        if n > 0:
            activate(n - 1, *chunks[n - 1])
    activate(len(chunks) - 1, *chunks[-1])


def last_kernel(kinds, n_dp, scale, x6, row_edges, edge_factors, up2, h6, gp2, w_one, w_up, *rest):
    kinds_ty, kinds_tx = kinds
    got_tx, rest = rest[:kinds_tx], rest[kinds_tx:]
    got_ty, rest = rest[:kinds_ty], rest[kinds_ty:]
    he, grad_pre_ref, keep_ref, send_ref, xe, ue, sums = rest
    count, breadth, _ = x6.shape
    wide, height = breadth + RIM, 2 * count
    channels = edge_factors.shape[2]
    me = lax.axis_index("dp")

    half = 3 * channels
    taps = 9
    c = channels
    near, far = 2, count - 2

    def flat(value):
        return value.reshape(-1, value.shape[-1])

    def joined(*values):
        return jnp.concatenate(values, axis=1)

    two = outer(
        flat(up2[near:far]), joined(flat(h6[near - 1 : far - 1]), flat(h6[near:far]))
    )
    (before, factor_before), (after, factor_after) = tx_sides(got_tx, height)
    got_rows = sides("ty", [ref[...].astype(F32) for ref in got_ty[::-1]])
    lines = []
    for side, planes in enumerate(got_rows):
        for array, target in enumerate((xe, ue)):
            for s in range(2):
                store_taps(target, 3 * side, s, planes[2 * array + s], wide)
                i = s if side == 0 else height - 2 + s
                rim = rim_of(
                    [before[2 * array + n][i : i + 1] for n in range(2)],
                    [after[2 * array + n][i : i + 1] for n in range(2)],
                )
                own = row_edges[2 * array + side, s].astype(F32)
                store_taps(target, 1 + side, s, jnp.concatenate([own, rim]), wide)
        outer_line = jnp.broadcast_to(planes[4][:, 0:1] + planes[4][:, 1:2], (wide, channels))
        i = 0 if side == 0 else height - 1
        ends = [
            jnp.broadcast_to(column[i : i + 1], (1, channels))
            for column in (factor_before, factor_after)
        ]
        rim = rim_of((None, ends[0]), (ends[1], None))
        inner_line = jnp.concatenate([edge_factors[side], rim])
        lines.append((outer_line, inner_line) if side == 0 else (inner_line, outer_line))

    def edge_conv(lines, weights):
        upper = jnp.concatenate([lines[0], lines[2]])
        lower = jnp.concatenate([lines[1], lines[3]])
        return deep_product(upper, lower, weights)

    pre = edge_conv(xe, w_one)
    grad = edge_conv(ue, w_up)
    one = outer(
        flat(gp2[near:far]),
        joined(
            flat(x6[near - 1 : far - 1, :, half:]),
            flat(x6[near:far]),
            flat(x6[near + 1 : far + 1, :, :half]),
        ),
    )
    inner_grads = []
    for side in range(2):
        rows = slice(side * wide, (side + 1) * wide)
        for t in range(2):
            lanes = slice(t * channels, (t + 1) * channels)
            hidden, grad_pre = activations(pre[rows, lanes], grad[rows, lanes], lines[side][t])
            grad_pre_ref[side, t] = grad_pre.astype(BF16)
            store_taps(he, side, t, hidden, breadth)
            if t != side:
                inner_grads.append(grad_pre[:breadth].astype(BF16))

    def ends(*values):
        return jnp.concatenate([flat(value) for value in values])

    two += outer(
        ends(up2[:near], up2[far:]),
        joined(
            ends(he[0], h6[: near - 1], h6[far - 1 :]),
            ends(h6[:near], h6[far:], he[1]),
        ),
    )
    one += outer(
        ends(
            joined(inner_grads[0], gp2[0, :, c:]),
            gp2[1:near],
            gp2[far : count - 1],
            joined(gp2[count - 1, :, :c], inner_grads[1]),
        ),
        joined(
            ends(xe[0, :breadth, half:], x6[: near - 1, :, half:], x6[far - 1 : count - 1, :, half:]),
            ends(x6[:near], x6[far:]),
            ends(x6[1 : near + 1, :, :half], x6[far + 1 :, :, :half], xe[3, :breadth, :half]),
        ),
    )

    def write(level_at, a, total):
        for e in range(3):
            part = (total[:, e * channels : (e + 1) * channels] * scale).astype(BF16)
            sums[level_at * taps + 3 * a + e] = part

    first, second = two[:, : 2 * half], two[:, 2 * half :]
    write(1, 0, first[:c, :half] + first[c:, half:])
    write(1, 1, first[:c, half:] + second[c:, :half])
    write(1, 2, second[:c, :half] + second[c:, half:])
    first, second, third = one[:, :half], one[:, half : 3 * half], one[:, 3 * half :]
    write(0, 0, first[:c] + second[c:, :half])
    write(0, 1, second[:c, :half] + second[c:, half:])
    write(0, 2, second[:c, half:] + third[c:])
    mine = keep_ref.shape[2]
    for partner in range(n_dp):
        slot = jnp.bitwise_xor(me, partner)
        target = send_ref if partner % 2 else keep_ref
        target[partner // 2] = sums[:, pl.ds(pl.multiple_of(slot * mine, mine), mine), :]


def output_kernel(middle, edges, filters, target, weights):
    count, breadth, _ = middle.shape
    channels = target.shape[3]
    pair_weights(weights, lambda a, e: jnp.transpose(filters[9 + 3 * a + e]))

    def write(result, at, pairs):
        for n in range(pairs):
            for t in range(2):
                target[0, 2 * (at + n) + t] = result[
                    n * breadth : (n + 1) * breadth, t * channels : (t + 1) * channels
                ]

    for at in range(0, count - 1, 2 * CHUNK):
        pairs = min(2 * CHUNK, count - 1 - at)
        write(pair_conv(middle, weights, at, pairs).astype(BF16), at + 1, pairs)
    upper = jnp.concatenate([edges[0], middle[count - 1]])
    lower = jnp.concatenate([middle[0], edges[1]])
    result = deep_product(upper, lower, weights)
    write(result[:breadth].astype(BF16), 0, 1)
    write(result[breadth:].astype(BF16), count, 1)


def grad_taps_kernel(kinds_tx, gp2, edges, filters, beside_pre, w_up, own_columns, *rest):
    got_tx, rest = rest[:kinds_tx], rest[kinds_tx:]
    taps6, weights, columns, beside6, beside_grad = rest
    pairs, breadth, _ = taps6.shape
    channels = columns.shape[2]
    pair_weights(weights, lambda a, e: filters[3 * (2 - a) + (2 - e)])
    beside = Beside(1, got_tx, own_columns, columns)
    grad = beside.conv(beside6, w_up)
    for t in range(2):
        lanes = slice(t * channels, (t + 1) * channels)
        _, beside_grad[t] = activations(beside_pre[:, lanes], grad[:, lanes], beside.factor(t))
    rims = rims_of(beside_grad, 0, pairs - 2, pairs - 1)
    for q in range(pairs - 2):
        for s in range(2):
            line = gp2[q + s, :, (1 - s) * channels : (2 - s) * channels].astype(F32)
            store_taps(taps6, q + 1, s, jnp.concatenate([line, rims[q][s]]), breadth)
    for side, q in enumerate((0, pairs - 1)):
        for s in range(2):
            store_taps(taps6, q, s, edges[side, s].astype(F32), breadth)


def grad_input_kernel(taps6, weights, target):
    pairs, breadth, _ = taps6.shape
    channels = target.shape[3]
    for at in range(0, pairs - 1, 2 * CHUNK):
        many = min(2 * CHUNK, pairs - 1 - at)
        result = pair_conv(taps6, weights, at, many).astype(BF16)
        for n in range(many):
            for t in range(2):
                target[0, 2 * (at + n) + t] = result[
                    n * breadth : (n + 1) * breadth, t * channels : (t + 1) * channels
                ]


def split_kernel(kept, got, own, *others):
    near = lax.axis_index("tx")
    far = 1 - near
    taps = own.shape[0]
    for target, half, at in zip((own,) + others, (near, near, far, far), (0, 1, 0, 1)):
        rows = pl.ds(half * taps, taps)
        target[...] = (kept[at, rows].astype(F32) + got[at, rows].astype(F32)).astype(BF16)


def total_kernel(*refs):
    total = refs[0][...].astype(F32)
    for ref in refs[1:-1]:
        total += ref[...].astype(F32)
    refs[-1][...] = total.astype(BF16)


def halves_kernel(own, by_both, by_x, by_y, one, two):
    first = lax.axis_index("tx") == 0
    near = own[...].astype(F32) + by_y[...].astype(F32)
    far = by_x[...].astype(F32) + by_both[...].astype(F32)
    one[...] = jnp.where(first, near, far)
    two[...] = jnp.where(first, far, near)


def add_kernel(more, kept, got, keep_ref, send_ref):
    for n in range(kept.shape[0]):
        total = (kept[n].astype(F32) + got[n].astype(F32)).astype(BF16)
        if more and n % 2:
            send_ref[n // 2] = total
        else:
            keep_ref[n // 2] = total


def sum_kernel(got, total_ref):
    total = got[0].astype(F32)
    for source in range(1, got.shape[0]):
        total += got[source].astype(F32)
    for copy in range(total_ref.shape[0]):
        total_ref[copy] = total.astype(BF16)


def partners(axis, bit):
    return [(i, i ^ bit) for i in range(lax.axis_size(axis))]


def total_by_swaps(kept, sent, run_between):
    sds = jax.ShapeDtypeStruct
    _, taps, mine, channels = kept.shape
    piece = sds((taps // 2, mine, channels), BF16)

    def total(*pieces):
        return pl.pallas_call(
            total_kernel,
            in_specs=[VMEM] * len(pieces),
            out_specs=VMEM,
            out_shape=piece,
            compiler_params=SMALL,
            name="sum_of_pieces",
        )(*pieces)

    got = lax.ppermute(sent, "dp", partners("dp", 1))
    own, by_y, by_x, by_both = pl.pallas_call(
        split_kernel,
        in_specs=[VMEM] * 2,
        out_specs=[VMEM] * 4,
        out_shape=[piece] * 4,
        compiler_params=SMALL,
        name="sum_on_chip",
    )(kept, got)
    both = [(2 * i + j, 2 * (i ^ 2) + (j ^ 1)) for i in range(4) for j in range(2)]
    got = [
        lax.ppermute(by_both, ("dp", "tx"), both),
        lax.ppermute(by_y, "dp", partners("dp", 2)),
        lax.ppermute(by_x, "tx", partners("tx", 1)),
    ]
    got = run_between(0, own, got)
    own = total(own, *got)
    got = run_between(1, own, [lax.ppermute(own, "ty", partners("ty", 2))])
    own = total(own, *got)
    both = [(2 * i + j, 2 * (i ^ 1) + (j ^ 1)) for i in range(4) for j in range(2)]
    got = [
        lax.ppermute(own, ("ty", "tx"), both),
        lax.ppermute(own, "tx", partners("tx", 1)),
        lax.ppermute(own, "ty", partners("ty", 1)),
    ]
    got = run_between(2, own, got)
    return pl.pallas_call(
        halves_kernel,
        in_specs=[VMEM] * 4,
        out_specs=[VMEM] * 2,
        out_shape=[sds(piece.shape, F32)] * 2,
        compiler_params=SMALL,
        name="both_halves",
    )(own, *got)


def total_by_groups(kept, sent, run_between):
    sds = jax.ShapeDtypeStruct
    _, taps, mine, channels = kept.shape
    n_dp = lax.axis_size("dp")
    bit = 1
    while bit < n_dp:
        got = lax.ppermute(sent, "dp", partners("dp", bit))
        half = kept.shape[0] // 2
        bit *= 2
        kept, sent = pl.pallas_call(
            functools.partial(add_kernel, bit < n_dp),
            in_specs=[VMEM] * 2,
            out_specs=[VMEM] * 2,
            out_shape=[sds((max(half, 1),) + kept.shape[1:], BF16)] * 2,
            compiler_params=SMALL,
            name="sum_of_crops",
        )(kept, got)
    tiles = lax.axis_size("ty") * lax.axis_size("tx")
    rows = taps * mine // tiles
    got = lax.all_to_all(kept.reshape(tiles, rows, channels), ("ty", "tx"), 0, 0, tiled=True)
    shared = pl.pallas_call(
        sum_kernel,
        in_specs=[VMEM],
        out_specs=VMEM,
        out_shape=sds((tiles, rows, channels), BF16),
        compiler_params=SMALL,
        name="sum_of_tiles",
    )(got)
    (total,) = run_between(0, shared, [lax.all_to_all(shared, ("ty", "tx"), 0, 0, tiled=True)])
    run_between(1, shared, [total])
    run_between(2, shared, [total])
    total = total.astype(F32).reshape(2, taps // 2, mine, channels)
    return total[0], total[1]


def on_device(features, filter_one, filter_two, speedup, land_mask, offsets, upstream):
    _, height, breadth, channels = features.shape
    mine = filter_one.shape[3]
    n_dp, n_ty, n_tx = (lax.axis_size(axis) for axis in ("dp", "ty", "tx"))
    kinds = kinds_ty, kinds_tx = min(2, n_ty - 1), min(2, n_tx - 1)
    taps = 9
    wide = breadth + RIM
    pairs = height // 2 + 1
    sds = jax.ShapeDtypeStruct

    one, two = (f.reshape(taps, channels, mine).transpose(0, 2, 1) for f in (filter_one, filter_two))
    *tx_sent, factor, shard, own_columns = pl.pallas_call(
        functools.partial(columns_kernel, kinds_tx),
        in_specs=[HBM] * 7,
        out_specs=[VMEM] * (kinds_tx + 3),
        out_shape=[pltpu.VMEM((4 * height + RIM, channels), BF16)] * kinds_tx
        + [pltpu.VMEM((height, breadth), F32), pltpu.VMEM((2 * taps, mine, channels), BF16)]
        + [pltpu.VMEM((4, height, channels), BF16)],
        scratch_shapes=[
            pltpu.VMEM((height * RIM, channels), F32),
            pltpu.VMEM((4, height, RIM, channels), BF16),
            pltpu.VMEM(speedup.shape, F32),
            pltpu.VMEM(land_mask.shape, jnp.int32),
            pltpu.SMEM(offsets.shape, jnp.int32),
            pltpu.SemaphoreType.DMA((9,)),
        ],
        compiler_params=SMALL,
        name="edge_columns",
    )(*in_hbm(offsets, features, upstream, speedup, land_mask, one, two))
    tx_got = swaps("tx", tx_sent)
    shards = [shard] + [
        lax.ppermute(shard, "dp", partners("dp", partner)) for partner in range(1, n_dp)
    ]

    count = height // 2
    k6 = 6 * channels
    x6, u6, up2, factors, edge_factors, row_edges = pl.pallas_call(
        own_kernel,
        in_specs=[HBM] * 2 + [VMEM],
        out_specs=[VMEM] * 6,
        out_shape=[
            pltpu.VMEM((count, breadth, k6), BF16),
            pltpu.VMEM((count, breadth, k6), BF16),
            pltpu.VMEM((count, breadth, 2 * channels), BF16),
            pltpu.VMEM((count - 1, 2, breadth, channels), F32),
            pltpu.VMEM((2, breadth, channels), F32),
            pltpu.VMEM((4, 2, breadth, channels), BF16),
        ],
        scratch_shapes=[
            pltpu.VMEM((2, height, breadth, channels), BF16),
            pltpu.SemaphoreType.DMA((2, 4)),
        ],
        compiler_params=SMALL,
        cost_estimate=pl.CostEstimate(flops=100000, bytes_accessed=100000, transcendentals=0),
        name="own_column_taps",
    )(*in_hbm(features, upstream), factor)
    row_edges, tx_got = lax.optimization_barrier((row_edges, tx_got))
    ty_sent = pl.pallas_call(
        functools.partial(rows_kernel, kinds_tx),
        in_specs=[VMEM] * (2 + kinds_tx),
        out_specs=[VMEM] * kinds_ty,
        out_shape=[pltpu.VMEM((PLANES, wide, channels), BF16)] * kinds_ty,
        compiler_params=SMALL,
        cost_estimate=pl.CostEstimate(flops=100000000000, bytes_accessed=100000000, transcendentals=0),
        name="edge_rows",
    )(row_edges, factor, *tx_got)
    ty_got = swaps("ty", ty_sent)

    weights = pltpu.VMEM((2, k6, 2 * channels), BF16)
    rows = CHUNK * breadth
    beside_scratch = [
        pltpu.VMEM((8, height + PAST, channels), F32),
        pltpu.VMEM((2, 2 * count, k6), BF16),
        pltpu.VMEM((2, 2 * count, channels), F32),
    ]
    x6, u6, h6, gp2, filters, w_one, w_up, beside_pre = pl.pallas_call(
        functools.partial(middle_kernel, kinds_tx, n_dp),
        in_specs=[VMEM] * (4 + kinds_tx + n_dp),
        out_specs=[VMEM] * 8,
        out_shape=[
            pltpu.VMEM(x6.shape, BF16),
            pltpu.VMEM(u6.shape, BF16),
            pltpu.VMEM((count - 1, breadth, k6), BF16),
            pltpu.VMEM((count, breadth, 2 * channels), BF16),
            pltpu.VMEM((2 * taps, channels, channels), BF16),
            weights,
            weights,
            pltpu.VMEM((2 * count, 2 * channels), F32),
        ],
        input_output_aliases={0: 0, 1: 1},
        scratch_shapes=beside_scratch
        + [
            pltpu.VMEM((count - 1, 2, RIM, channels), F32),
            pltpu.VMEM((4, height, channels), F32),
        ]
        + [pltpu.VMEM((rows, 2 * channels), F32)] * 4,
        compiler_params=pltpu.CompilerParams(vmem_limit_bytes=20 * MIB),
        cost_estimate=pl.CostEstimate(
            flops=2 * 18 * height * breadth * channels * channels,
            bytes_accessed=20 * MIB,
            transcendentals=height * breadth * channels,
        ),
        name="middle_rows",
    )(x6, u6, own_columns, factors, *tx_got, *shards)

    scale = 1.0 / math.sqrt(height * breadth * n_dp * n_ty * n_tx)
    h6_edges, grad_pre_edges, kept, sent = pl.pallas_call(
        functools.partial(last_kernel, kinds, n_dp, scale),
        in_specs=[VMEM] * (8 + kinds_tx + kinds_ty),
        out_specs=[VMEM] * 4,
        out_shape=[
            pltpu.VMEM((2, breadth, k6), BF16),
            pltpu.VMEM((2, 2, wide, channels), BF16),
            pltpu.VMEM((n_dp // 2, 2 * taps, mine, channels), BF16),
            pltpu.VMEM((n_dp // 2, 2 * taps, mine, channels), BF16),
        ],
        scratch_shapes=[
            pltpu.VMEM((4, wide, k6), BF16),
            pltpu.VMEM((4, wide, k6), BF16),
            pltpu.VMEM((2 * taps, channels, channels), BF16),
        ],
        compiler_params=pltpu.CompilerParams(vmem_limit_bytes=20 * MIB),
        name="outer_rows_and_filter_grads",
    )(x6, row_edges, edge_factors, up2, h6, gp2, w_one, w_up, *tx_got, *ty_got[::-1])

    def conv_cost(macs):
        return pl.CostEstimate(
            flops=18 * macs * height * breadth * channels * channels,
            bytes_accessed=4 * height * breadth * channels,
            transcendentals=0,
        )

    def output_step(ready):
        h6_now, _ = lax.optimization_barrier((h6_edges, ready))
        return pl.pallas_call(
            output_kernel,
            in_specs=[VMEM] * 3,
            out_specs=VMEM,
            out_shape=sds(features.shape, BF16),
            scratch_shapes=[weights],
            compiler_params=MEDIUM,
            cost_estimate=conv_cost(1),
            name="output",
        )(h6, h6_now, filters)

    def taps_step(ready):
        edges, _ = lax.optimization_barrier((grad_pre_edges, ready))
        return pl.pallas_call(
            functools.partial(grad_taps_kernel, kinds_tx),
            in_specs=[VMEM] * (6 + kinds_tx),
            out_specs=[VMEM] * 2,
            out_shape=[pltpu.VMEM((pairs, breadth, k6), BF16), weights],
            scratch_shapes=beside_scratch,
            compiler_params=MEDIUM,
            cost_estimate=conv_cost(0),
            name="grad_pre_taps",
        )(gp2, edges, filters, beside_pre, w_up, own_columns, *tx_got)

    def grad_input_step(ready):
        g6, w_back = results.pop()
        g6, _ = lax.optimization_barrier((g6, ready))
        return pl.pallas_call(
            grad_input_kernel,
            in_specs=[VMEM] * 2,
            out_specs=VMEM,
            out_shape=sds(features.shape, BF16),
            compiler_params=MEDIUM,
            cost_estimate=conv_cost(1),
            name="grad_input",
        )(g6, w_back)

    results = []

    def run_between(which, ready, got):
        result = (output_step, taps_step, grad_input_step)[which](ready)
        result, got = lax.optimization_barrier((result, got))
        results.append(result)
        return got

    if (n_dp, n_ty, n_tx) == (4, 4, 2):
        grads = total_by_swaps(kept, sent, run_between)
    else:
        grads = total_by_groups(kept, sent, run_between)
    grads = [g.reshape(3, 3, mine, channels).transpose(0, 1, 3, 2) for g in grads]
    return results[0], results[1], grads[0], grads[1]


def solution(mesh):
    in_specs = (
        P("dp", "ty", "tx", None),
        P(None, None, None, "dp"),
        P(None, None, None, "dp"),
        P("dp", "ty", "tx"),
        P("dp", "ty", "tx"),
        P("dp", None),
        P("dp", "ty", "tx", None),
    )
    out_specs = (
        P("dp", "ty", "tx", None),
        P("dp", "ty", "tx", None),
        P(None, None, None, "dp"),
        P(None, None, None, "dp"),
    )
    return jax.shard_map(
        on_device, mesh=mesh, in_specs=in_specs, out_specs=out_specs, check_vma=False
    )
```

```python
import functools
import math

import jax
import jax.numpy as jnp
from jax import lax
from jax.experimental import pallas as pl
from jax.experimental.pallas import tpu as pltpu
from jax.sharding import PartitionSpec as P

F32 = jnp.float32
BF16 = jnp.bfloat16
RIM = 16
PAST = 8
CHUNK = 16
PLANES = 5
VMEM = pl.BlockSpec(memory_space=pltpu.VMEM)
HBM = pl.BlockSpec(memory_space=pltpu.HBM)
MIB = 1024 * 1024
SMALL = pltpu.CompilerParams(vmem_limit_bytes=8 * MIB)
MEDIUM = pltpu.CompilerParams(vmem_limit_bytes=16 * MIB)


def in_hbm(*arrays):
    return [pltpu.with_memory_space_constraint(array, pltpu.HBM) for array in arrays]


def is_odd(axis):
    return lax.rem(lax.axis_index(axis), 2) == 1


def kind_pairs(count, kind):
    return [(i, i + 1) for i in range(kind, count - 1, 2)]


def swaps(axis, sent):
    got = []
    for kind in reversed(range(len(sent))):
        pairs = [p for i, j in kind_pairs(lax.axis_size(axis), kind) for p in ((i, j), (j, i))]
        got.append(lax.ppermute(sent[kind], axis, pairs))
    return got[::-1]


def sides(axis, got):
    odd = is_odd(axis)
    first = got[0]
    second = got[1] if len(got) > 1 else jnp.zeros_like(first)
    return jnp.where(odd, first, second), jnp.where(odd, second, first)


def rim_of(before, after):
    channels = after[0].shape[1]
    at = lax.broadcasted_iota(jnp.int32, (RIM, channels), 0)
    rim = jnp.where(at == 0, after[0], 0.0)
    if after[1] is not None:
        rim = jnp.where(at == 1, after[1], rim)
    if before[0] is not None:
        rim = jnp.where(at == RIM - 2, before[0], rim)
    return jnp.where(at == RIM - 1, before[1], rim)


def factor_tile(line, channels):
    high = line.astype(BF16).astype(F32)
    low = (line - high).astype(BF16).astype(F32)
    line = jnp.concatenate([high, low, jnp.zeros((RIM - 2, line.shape[1]), F32)])
    past = channels - line.shape[1]
    return line if past == 0 else jnp.concatenate([line, jnp.zeros((RIM, past), F32)], axis=1)


def tx_sides(got, height):
    result = []
    for rows in sides("tx", [ref[...].astype(F32) for ref in got]):
        lines = [rows[n * height : (n + 1) * height] for n in range(4)]
        parts = jnp.transpose(rows[4 * height :])
        result.append((lines, parts[:height, 0:1] + parts[:height, 1:2]))
    return result


def two_parts(column, channels):
    high = column.astype(BF16).astype(F32)
    low = (column - high).astype(BF16).astype(F32)
    lane = lax.broadcasted_iota(jnp.int32, (column.shape[0], channels), 1)
    return jnp.where(lane == 0, high, jnp.where(lane == 1, low, 0.0))


def columns_kernel(kinds_tx, offsets, features, upstream, speedup, land, one, two, *rest):
    sent, rest = rest[:kinds_tx], rest[kinds_tx:]
    factor_ref, filters_ref, own_columns, spread, blocks, speed, mask, place, sems = rest
    _, height, breadth = speedup.shape
    channels = features.shape[3]
    taps = one.shape[0]
    ends = (pl.ds(0, RIM), pl.ds(breadth - RIM, RIM))
    moves = [(speedup, speed), (land, mask), (offsets, place)]
    moves += [
        (ref.at[0, :, ends[side], :], blocks.at[2 * array + side])
        for array, ref in enumerate((features, upstream))
        for side in range(2)
    ]
    moves += [(one, filters_ref.at[pl.ds(0, taps)]), (two, filters_ref.at[pl.ds(taps, taps)])]
    copies = [pltpu.make_async_copy(*move, sems.at[n]) for n, move in enumerate(moves)]
    for copy in copies:
        copy.start()
    for copy in copies[:3]:
        copy.wait()
    shape = (height, breadth)
    row = place[0, 0] + lax.axis_index("ty") * height + lax.broadcasted_iota(jnp.int32, shape, 0)
    col = place[0, 1] + lax.axis_index("tx") * breadth + lax.broadcasted_iota(jnp.int32, shape, 1)
    factor = jnp.where(mask[0] == 1, speed[0], jnp.float32(1.0))
    factor = factor / (1.0 + row.astype(F32) / 512.0) / (1.0 + col.astype(F32) / 1024.0)
    factor_ref[...] = factor
    odd = is_odd("tx")

    def column(at):
        return spread[pl.ds(at, height, stride=RIM), :]

    heads, tails = [], []
    for array in range(2):
        copies[3 + 2 * array].wait()
        spread[...] = blocks[2 * array].astype(F32).reshape(height * RIM, channels)
        heads += [column(0), column(1)]
        copies[4 + 2 * array].wait()
        spread[...] = blocks[2 * array + 1].astype(F32).reshape(height * RIM, channels)
        tails += [column(RIM - 2), column(RIM - 1)]
    across = jnp.transpose(factor)
    heads.append(factor_tile(across[:1], channels))
    tails.append(factor_tile(across[breadth - 1 :], channels))
    for plane in range(PLANES):
        rows = slice(plane * height, min((plane + 1) * height, sent[0].shape[0]))
        sent[0][rows] = jnp.where(odd, heads[plane], tails[plane]).astype(BF16)
        if kinds_tx == 2:
            sent[1][rows] = jnp.where(odd, tails[plane], heads[plane]).astype(BF16)
    for array in range(2):
        own_columns[2 * array] = heads[2 * array].astype(BF16)
        own_columns[2 * array + 1] = tails[2 * array + 1].astype(BF16)
    for copy in copies[7:]:
        copy.wait()


def rows_kernel(kinds_tx, edges, factor_ref, *rest):
    got, sent = rest[:kinds_tx], rest[kinds_tx:]
    height, breadth = factor_ref.shape
    channels = edges.shape[3]
    across = jnp.transpose(factor_ref[...])
    (before, factor_before), (after, factor_after) = tx_sides(got, height)

    def message(side, lines, edge):
        planes = []
        for array in range(2):
            for n, line in enumerate(lines):
                rim = rim_of(
                    [before[2 * array + i][line : line + 1] for i in range(2)],
                    [after[2 * array + i][line : line + 1] for i in range(2)],
                )
                planes.append(jnp.concatenate([edges[2 * array + side, n].astype(F32), rim]))
        own = two_parts(across[:, edge : edge + 1], channels)
        rim = rim_of(
            (None, two_parts(factor_before[edge : edge + 1], channels)),
            (two_parts(factor_after[edge : edge + 1], channels), None),
        )
        planes.append(jnp.concatenate([own, rim]))
        return planes

    heads = message(0, (0, 1), 0)
    tails = message(1, (height - 2, height - 1), height - 1)
    odd = is_odd("ty")
    for plane in range(PLANES):
        sent[0][plane] = jnp.where(odd, heads[plane], tails[plane]).astype(BF16)
        if len(sent) == 2:
            sent[1][plane] = jnp.where(odd, tails[plane], heads[plane]).astype(BF16)


def pair_weights(target, block_of):
    channels = target.shape[2] // 2
    for half in range(2):
        for s in range(2):
            for t in range(2):
                a = 2 * half + s - t
                for e in range(3):
                    block = block_of(a, e) if 0 <= a <= 2 else jnp.zeros((channels, channels), BF16)
                    at = (3 * s + e) * channels
                    target[half, at : at + channels, t * channels : (t + 1) * channels] = block


def store_taps(target, where, s, wide, width):
    channels = wide.shape[-1]
    axis = wide.ndim - 2
    for e in range(3):
        if e == 1:
            moved = wide
        else:
            moved = pltpu.roll(wide, 1 if e == 0 else wide.shape[axis] - 1, axis)
        moved = moved[..., :width, :].astype(BF16)
        target[where, :, (3 * s + e) * channels : (3 * s + e + 1) * channels] = moved


def pair_conv(source, weights, at, pairs):
    _, width, depth = source.shape
    upper = source[at : at + pairs].reshape(pairs * width, depth)
    lower = source[at + 1 : at + 1 + pairs].reshape(pairs * width, depth)
    return deep_product(upper, lower, weights)


def deep_product(upper, lower, weights):
    _, depth, lanes = weights.shape
    return jnp.dot(
        jnp.concatenate([upper, lower], axis=1),
        weights[...].reshape(2 * depth, lanes),
        preferred_element_type=F32,
    )


def outer(grads, source):
    return lax.dot_general(grads, source, (((0,), (0,)), ((), ())), preferred_element_type=F32)


def own_kernel(
    features, upstream, factor_ref, x6, u6, up2, factors, edge_factors, edges, cells, sems
):
    _, height, breadth, channels = features.shape
    arrays = (features, upstream)
    parts = sems.shape[1]
    rows = height // parts
    copies = [
        [
            pltpu.make_async_copy(
                ref.at[0, pl.ds(n * rows, rows)],
                cells.at[array, pl.ds(n * rows, rows)],
                sems.at[array, n],
            )
            for array, ref in enumerate(arrays)
        ]
        for n in range(parts)
    ]
    for pair in copies:
        for copy in pair:
            copy.start()
    across = jnp.transpose(factor_ref[...])
    for i in range(height):
        line = jnp.broadcast_to(across[:, i : i + 1], (breadth, channels))
        if i in (0, height - 1):
            edge_factors[min(i, 1)] = line
        else:
            factors[(i - 1) // 2, (i - 1) % 2] = line

    def spread(q, carry):
        for s in range(2):
            for array, target in enumerate((x6, u6)):
                line = cells[array, 2 * q + s]
                store_taps(target, q, s, line.astype(F32), breadth)
            up2[q, :, s * channels : (s + 1) * channels] = line
        return carry

    for n, pair in enumerate(copies):
        for copy in pair:
            copy.wait()
        lax.fori_loop(n * rows // 2, (n + 1) * rows // 2, spread, 0)
    for array in range(2):
        edges[2 * array] = cells[array, :2]
        edges[2 * array + 1] = cells[array, height - 2 :]


def activations(pre, grad, factor):
    s = 0.5 * jnp.tanh(0.5 * pre) + 0.5
    fs = factor * s
    return pre * fs, grad * fs * (1.0 + pre * (1.0 - s))


class Beside:
    def __init__(self, array, got_tx, own_columns, columns):
        channels = columns.shape[2]
        height = columns.shape[1] - PAST
        self.array, self.columns, self.count = array, columns, height // 2
        (before, factor_before), (after, factor_after) = tx_sides(got_tx, height)
        own = own_columns[...].astype(F32)
        lines = (
            before[2 * array],
            before[2 * array + 1],
            own[2 * array],
            own[2 * array + 1],
            after[2 * array],
            after[2 * array + 1],
            jnp.broadcast_to(factor_before, (height, channels)),
            jnp.broadcast_to(factor_after, (height, channels)),
        )
        for n, line in enumerate(lines):
            columns[n, :height] = line
        columns[:, height:] = jnp.zeros((len(lines), PAST, channels), F32)

    def rows(self, n, begin):
        return self.columns[n, pl.ds(begin, self.count, stride=2), :]

    def conv(self, taps6, weights):
        count, channels = self.count, self.columns.shape[2]
        for half in range(2):
            for s in range(2):
                for side in range(2):
                    for e in range(3):
                        at = (3 * s + e) * channels
                        taps6[half, side * count : (side + 1) * count, at : at + channels] = (
                            self.rows(3 * side + e, 2 * half + s).astype(BF16)
                        )
        return deep_product(taps6[0], taps6[1], weights)

    def factor(self, t):
        return jnp.concatenate([self.rows(6, 1 + t), self.rows(7, 1 + t)])


def rims_of(lines, begin, pairs, count):
    return [
        [
            rim_of((None, lines[t, m : m + 1, :]), (lines[t, count + m : count + m + 1, :], None))
            for t in range(2)
        ]
        for m in range(begin, begin + pairs)
    ]


def middle_kernel(kinds_tx, n_dp, x6_in, u6_in, own_columns, factors, *rest):
    got_tx, rest = rest[:kinds_tx], rest[kinds_tx:]
    shards, rest = rest[n_dp - 2 : n_dp] + rest[: n_dp - 2], rest[n_dp:]
    x6, u6, h6, gp2, filters_ref, w_one, w_up, beside_pre = rest[:8]
    columns, beside6, beside_hidden, hidden_rims, edge_cells = rest[8:13]
    pres, grads = rest[13:15], rest[15:17]
    count, breadth, _ = x6.shape
    channels = columns.shape[2]
    mine = shards[0].shape[1]
    me = lax.axis_index("dp")
    for partner, shard in enumerate(shards):
        slot = jnp.bitwise_xor(me, partner)
        filters_ref[:, pl.ds(pl.multiple_of(slot * mine, mine), mine), :] = shard[...]
    pair_weights(w_one, lambda a, e: jnp.transpose(filters_ref[3 * a + e]))
    (before, _), (after, _) = tx_sides(got_tx, 2 * count)
    for array in range(2):
        edge_cells[2 * array] = before[2 * array + 1]
        edge_cells[2 * array + 1] = after[2 * array]
    spot = lax.broadcasted_iota(jnp.int32, (RIM, channels), 0)
    first, last = slice(0, RIM), slice(breadth - RIM, breadth)

    def patch(array, begin, end):
        source, target = ((x6_in, x6), (u6_in, u6))[array]
        for q in range(begin, end):
            for s in range(2):
                i = 2 * q + s
                for e, rows, at in ((0, first, 0), (2, last, RIM - 1)):
                    cell = edge_cells[2 * array + e // 2, i : i + 1, :]
                    lanes = slice((3 * s + e) * channels, (3 * s + e + 1) * channels)
                    value = jnp.where(spot == at, cell, source[q, rows, lanes].astype(F32))
                    target[q, rows, lanes] = value.astype(BF16)

    def convolve(n, at, pairs):
        rows = pairs * breadth
        pres[n % 2][:rows] = pair_conv(x6, w_one, at, pairs)
        grads[n % 2][:rows] = pair_conv(u6, w_up, at, pairs)

    def activate(n, at, pairs):
        rows = pairs * breadth
        here = slice(at, at + pairs)
        for t in range(2):
            lanes = slice(t * channels, (t + 1) * channels)
            hidden, grad_pre = activations(
                pres[n % 2][:rows, lanes],
                grads[n % 2][:rows, lanes],
                factors[here, t].reshape(rows, channels),
            )
            hidden = hidden.reshape(pairs, breadth, channels)
            grad_pre = grad_pre.astype(BF16).reshape(pairs, breadth, channels)
            store_taps(
                h6, here, t, jnp.concatenate([hidden, hidden_rims[here, t]], axis=1), breadth
            )
            gp2[at + t : at + t + pairs, :, (1 - t) * channels : (2 - t) * channels] = grad_pre

    chunks = [(0, 0)]
    while sum(chunks[-1]) < count - 1:
        left = count - 1 - sum(chunks[-1])
        chunks.append((sum(chunks[-1]), min(left, CHUNK, max(3, (left + 1) // 2))))
    del chunks[0]
    done = 0
    for n, (at, pairs) in enumerate(chunks):
        for array in range(2):
            patch(array, done, at + pairs + 1)
        done = at + pairs + 1
        if n == 0:
            pair_weights(w_up, lambda a, e: filters_ref[9 + 3 * (2 - a) + (2 - e)])
        convolve(n, at, pairs)
        if n == 0:
            beside = Beside(0, got_tx, own_columns, columns)
            beside_pre[...] = beside.conv(beside6, w_one)
            for t in range(2):
                lanes = slice(t * channels, (t + 1) * channels)
                beside_hidden[t], _ = activations(beside_pre[:, lanes], 0.0, beside.factor(t))
        for m, rims in enumerate(rims_of(beside_hidden, at, pairs, count)):
            for t in range(2):
                hidden_rims[at + m, t] = rims[t]
        if n > 0:
            activate(n - 1, *chunks[n - 1])
    activate(len(chunks) - 1, *chunks[-1])


def last_kernel(kinds, n_dp, scale, x6, row_edges, edge_factors, up2, h6, gp2, w_one, w_up, *rest):
    kinds_ty, kinds_tx = kinds
    got_tx, rest = rest[:kinds_tx], rest[kinds_tx:]
    got_ty, rest = rest[:kinds_ty], rest[kinds_ty:]
    he, grad_pre_ref, keep_ref, send_ref, xe, ue, sums = rest
    count, breadth, _ = x6.shape
    wide, height = breadth + RIM, 2 * count
    channels = edge_factors.shape[2]
    me = lax.axis_index("dp")

    half = 3 * channels
    taps = 9
    c = channels
    near, far = 2, count - 2

    def flat(value):
        return value.reshape(-1, value.shape[-1])

    def joined(*values):
        return jnp.concatenate(values, axis=1)

    two = outer(
        flat(up2[near:far]), joined(flat(h6[near - 1 : far - 1]), flat(h6[near:far]))
    )
    (before, factor_before), (after, factor_after) = tx_sides(got_tx, height)
    got_rows = sides("ty", [ref[...].astype(F32) for ref in got_ty])
    lines = []
    for side, planes in enumerate(got_rows):
        for array, target in enumerate((xe, ue)):
            for s in range(2):
                store_taps(target, 3 * side, s, planes[2 * array + s], wide)
                i = s if side == 0 else height - 2 + s
                rim = rim_of(
                    [before[2 * array + n][i : i + 1] for n in range(2)],
                    [after[2 * array + n][i : i + 1] for n in range(2)],
                )
                own = row_edges[2 * array + side, s].astype(F32)
                store_taps(target, 1 + side, s, jnp.concatenate([own, rim]), wide)
        outer_line = jnp.broadcast_to(planes[4][:, 0:1] + planes[4][:, 1:2], (wide, channels))
        i = 0 if side == 0 else height - 1
        ends = [
            jnp.broadcast_to(column[i : i + 1], (1, channels))
            for column in (factor_before, factor_after)
        ]
        rim = rim_of((None, ends[0]), (ends[1], None))
        inner_line = jnp.concatenate([edge_factors[side], rim])
        lines.append((outer_line, inner_line) if side == 0 else (inner_line, outer_line))

    def edge_conv(lines, weights):
        upper = jnp.concatenate([lines[0], lines[2]])
        lower = jnp.concatenate([lines[1], lines[3]])
        return deep_product(upper, lower, weights)

    pre = edge_conv(xe, w_one)
    grad = edge_conv(ue, w_up)
    one = outer(
        flat(gp2[near:far]),
        joined(
            flat(x6[near - 1 : far - 1, :, half:]),
            flat(x6[near:far]),
            flat(x6[near + 1 : far + 1, :, :half]),
        ),
    )
    inner_grads = []
    for side in range(2):
        rows = slice(side * wide, (side + 1) * wide)
        for t in range(2):
            lanes = slice(t * channels, (t + 1) * channels)
            hidden, grad_pre = activations(pre[rows, lanes], grad[rows, lanes], lines[side][t])
            grad_pre_ref[side, t] = grad_pre.astype(BF16)
            store_taps(he, side, t, hidden, breadth)
            if t != side:
                inner_grads.append(grad_pre[:breadth].astype(BF16))

    def ends(*values):
        return jnp.concatenate([flat(value) for value in values])

    two += outer(
        ends(up2[:near], up2[far:]),
        joined(
            ends(he[0], h6[: near - 1], h6[far - 1 :]),
            ends(h6[:near], h6[far:], he[1]),
        ),
    )
    one += outer(
        ends(
            joined(inner_grads[0], gp2[0, :, c:]),
            gp2[1:near],
            gp2[far : count - 1],
            joined(gp2[count - 1, :, :c], inner_grads[1]),
        ),
        joined(
            ends(xe[0, :breadth, half:], x6[: near - 1, :, half:], x6[far - 1 : count - 1, :, half:]),
            ends(x6[:near], x6[far:]),
            ends(x6[1 : near + 1, :, :half], x6[far + 1 :, :, :half], xe[3, :breadth, :half]),
        ),
    )

    def write(level_at, a, total):
        for e in range(3):
            part = (total[:, e * channels : (e + 1) * channels] * scale).astype(BF16)
            sums[level_at * taps + 3 * a + e] = part

    first, second = two[:, : 2 * half], two[:, 2 * half :]
    write(1, 0, first[:c, :half] + first[c:, half:])
    write(1, 1, first[:c, half:] + second[c:, :half])
    write(1, 2, second[:c, :half] + second[c:, half:])
    first, second, third = one[:, :half], one[:, half : 3 * half], one[:, 3 * half :]
    write(0, 0, first[:c] + second[c:, :half])
    write(0, 1, second[:c, :half] + second[c:, half:])
    write(0, 2, second[:c, half:] + third[c:])
    mine = keep_ref.shape[2]
    for partner in range(n_dp):
        slot = jnp.bitwise_xor(me, partner)
        target = send_ref if partner % 2 else keep_ref
        target[partner // 2] = sums[:, pl.ds(pl.multiple_of(slot * mine, mine), mine), :]


def output_kernel(middle, edges, filters, target, weights):
    count, breadth, _ = middle.shape
    channels = target.shape[3]
    pair_weights(weights, lambda a, e: jnp.transpose(filters[9 + 3 * a + e]))

    def write(result, at, pairs):
        for n in range(pairs):
            for t in range(2):
                target[0, 2 * (at + n) + t] = result[
                    n * breadth : (n + 1) * breadth, t * channels : (t + 1) * channels
                ]

    for at in range(0, count - 1, 2 * CHUNK):
        pairs = min(2 * CHUNK, count - 1 - at)
        write(pair_conv(middle, weights, at, pairs).astype(BF16), at + 1, pairs)
    upper = jnp.concatenate([edges[0], middle[count - 1]])
    lower = jnp.concatenate([middle[0], edges[1]])
    result = deep_product(upper, lower, weights)
    write(result[:breadth].astype(BF16), 0, 1)
    write(result[breadth:].astype(BF16), count, 1)


def grad_taps_kernel(kinds_tx, gp2, edges, filters, beside_pre, w_up, own_columns, *rest):
    got_tx, rest = rest[:kinds_tx], rest[kinds_tx:]
    taps6, weights, columns, beside6, beside_grad = rest
    pairs, breadth, _ = taps6.shape
    channels = columns.shape[2]
    pair_weights(weights, lambda a, e: filters[3 * (2 - a) + (2 - e)])
    beside = Beside(1, got_tx, own_columns, columns)
    grad = beside.conv(beside6, w_up)
    for t in range(2):
        lanes = slice(t * channels, (t + 1) * channels)
        _, beside_grad[t] = activations(beside_pre[:, lanes], grad[:, lanes], beside.factor(t))
    rims = rims_of(beside_grad, 0, pairs - 2, pairs - 1)
    for q in range(pairs - 2):
        for s in range(2):
            line = gp2[q + s, :, (1 - s) * channels : (2 - s) * channels].astype(F32)
            store_taps(taps6, q + 1, s, jnp.concatenate([line, rims[q][s]]), breadth)
    for side, q in enumerate((0, pairs - 1)):
        for s in range(2):
            store_taps(taps6, q, s, edges[side, s].astype(F32), breadth)


def grad_input_kernel(taps6, weights, target):
    pairs, breadth, _ = taps6.shape
    channels = target.shape[3]
    for at in range(0, pairs - 1, 2 * CHUNK):
        many = min(2 * CHUNK, pairs - 1 - at)
        result = pair_conv(taps6, weights, at, many).astype(BF16)
        for n in range(many):
            for t in range(2):
                target[0, 2 * (at + n) + t] = result[
                    n * breadth : (n + 1) * breadth, t * channels : (t + 1) * channels
                ]


def split_kernel(kept, got, own, *others):
    near = lax.axis_index("tx")
    far = 1 - near
    taps = own.shape[0]
    for target, half, at in zip((own,) + others, (near, near, far, far), (0, 1, 0, 1)):
        rows = pl.ds(half * taps, taps)
        target[...] = (kept[at, rows].astype(F32) + got[at, rows].astype(F32)).astype(BF16)


def total_kernel(*refs):
    total = refs[0][...].astype(F32)
    for ref in refs[1:-1]:
        total += ref[...].astype(F32)
    refs[-1][...] = total.astype(BF16)


def halves_kernel(own, by_both, by_x, by_y, one, two):
    first = lax.axis_index("tx") == 0
    near = own[...].astype(F32) + by_y[...].astype(F32)
    far = by_x[...].astype(F32) + by_both[...].astype(F32)
    one[...] = jnp.where(first, near, far)
    two[...] = jnp.where(first, far, near)


def add_kernel(more, kept, got, keep_ref, send_ref):
    for n in range(kept.shape[0]):
        total = (kept[n].astype(F32) + got[n].astype(F32)).astype(BF16)
        if more and n % 2:
            send_ref[n // 2] = total
        else:
            keep_ref[n // 2] = total


def sum_kernel(got, total_ref):
    total = got[0].astype(F32)
    for source in range(1, got.shape[0]):
        total += got[source].astype(F32)
    for copy in range(total_ref.shape[0]):
        total_ref[copy] = total.astype(BF16)


def partners(axis, bit):
    return [(i, i ^ bit) for i in range(lax.axis_size(axis))]


def total_by_swaps(kept, sent, run_between):
    sds = jax.ShapeDtypeStruct
    _, taps, mine, channels = kept.shape
    piece = sds((taps // 2, mine, channels), BF16)

    def total(*pieces):
        return pl.pallas_call(
            total_kernel,
            in_specs=[VMEM] * len(pieces),
            out_specs=VMEM,
            out_shape=piece,
            compiler_params=SMALL,
            name="sum_of_pieces",
        )(*pieces)

    got = lax.ppermute(sent, "dp", partners("dp", 1))
    own, by_y, by_x, by_both = pl.pallas_call(
        split_kernel,
        in_specs=[VMEM] * 2,
        out_specs=[VMEM] * 4,
        out_shape=[piece] * 4,
        compiler_params=SMALL,
        name="sum_on_chip",
    )(kept, got)
    both = [(2 * i + j, 2 * (i ^ 2) + (j ^ 1)) for i in range(4) for j in range(2)]
    got = [
        lax.ppermute(by_both, ("dp", "tx"), both),
        lax.ppermute(by_y, "dp", partners("dp", 2)),
        lax.ppermute(by_x, "tx", partners("tx", 1)),
    ]
    got = run_between(0, own, got)
    own = total(own, *got)
    got = run_between(1, own, [lax.ppermute(own, "ty", partners("ty", 2))])
    own = total(own, *got)
    both = [(2 * i + j, 2 * (i ^ 1) + (j ^ 1)) for i in range(4) for j in range(2)]
    got = [
        lax.ppermute(own, ("ty", "tx"), both),
        lax.ppermute(own, "tx", partners("tx", 1)),
        lax.ppermute(own, "ty", partners("ty", 1)),
    ]
    got = run_between(2, own, got)
    return pl.pallas_call(
        halves_kernel,
        in_specs=[VMEM] * 4,
        out_specs=[VMEM] * 2,
        out_shape=[sds(piece.shape, F32)] * 2,
        compiler_params=SMALL,
        name="both_halves",
    )(own, *got)


def total_by_groups(kept, sent, run_between):
    sds = jax.ShapeDtypeStruct
    _, taps, mine, channels = kept.shape
    n_dp = lax.axis_size("dp")
    bit = 1
    while bit < n_dp:
        got = lax.ppermute(sent, "dp", partners("dp", bit))
        half = kept.shape[0] // 2
        bit *= 2
        kept, sent = pl.pallas_call(
            functools.partial(add_kernel, bit < n_dp),
            in_specs=[VMEM] * 2,
            out_specs=[VMEM] * 2,
            out_shape=[sds((max(half, 1),) + kept.shape[1:], BF16)] * 2,
            compiler_params=SMALL,
            name="sum_of_crops",
        )(kept, got)
    tiles = lax.axis_size("ty") * lax.axis_size("tx")
    rows = taps * mine // tiles
    got = lax.all_to_all(kept.reshape(tiles, rows, channels), ("ty", "tx"), 0, 0, tiled=True)
    shared = pl.pallas_call(
        sum_kernel,
        in_specs=[VMEM],
        out_specs=VMEM,
        out_shape=sds((tiles, rows, channels), BF16),
        compiler_params=SMALL,
        name="sum_of_tiles",
    )(got)
    (total,) = run_between(0, shared, [lax.all_to_all(shared, ("ty", "tx"), 0, 0, tiled=True)])
    run_between(1, shared, [total])
    run_between(2, shared, [total])
    total = total.astype(F32).reshape(2, taps // 2, mine, channels)
    return total[0], total[1]


def on_device(features, filter_one, filter_two, speedup, land_mask, offsets, upstream):
    _, height, breadth, channels = features.shape
    mine = filter_one.shape[3]
    n_dp, n_ty, n_tx = (lax.axis_size(axis) for axis in ("dp", "ty", "tx"))
    kinds = kinds_ty, kinds_tx = min(2, n_ty - 1), min(2, n_tx - 1)
    taps = 9
    wide = breadth + RIM
    pairs = height // 2 + 1
    sds = jax.ShapeDtypeStruct

    one, two = (f.reshape(taps, channels, mine).transpose(0, 2, 1) for f in (filter_one, filter_two))
    *tx_sent, factor, shard, own_columns = pl.pallas_call(
        functools.partial(columns_kernel, kinds_tx),
        in_specs=[HBM] * 7,
        out_specs=[VMEM] * (kinds_tx + 3),
        out_shape=[pltpu.VMEM((4 * height + RIM, channels), BF16)] * kinds_tx
        + [pltpu.VMEM((height, breadth), F32), pltpu.VMEM((2 * taps, mine, channels), BF16)]
        + [pltpu.VMEM((4, height, channels), BF16)],
        scratch_shapes=[
            pltpu.VMEM((height * RIM, channels), F32),
            pltpu.VMEM((4, height, RIM, channels), BF16),
            pltpu.VMEM(speedup.shape, F32),
            pltpu.VMEM(land_mask.shape, jnp.int32),
            pltpu.SMEM(offsets.shape, jnp.int32),
            pltpu.SemaphoreType.DMA((9,)),
        ],
        compiler_params=SMALL,
        name="edge_columns",
    )(*in_hbm(offsets, features, upstream, speedup, land_mask, one, two))
    tx_got = swaps("tx", tx_sent)
    shards = [shard] + [
        lax.ppermute(shard, "dp", partners("dp", partner)) for partner in range(1, n_dp)
    ]

    count = height // 2
    k6 = 6 * channels
    x6, u6, up2, factors, edge_factors, row_edges = pl.pallas_call(
        own_kernel,
        in_specs=[HBM] * 2 + [VMEM],
        out_specs=[VMEM] * 6,
        out_shape=[
            pltpu.VMEM((count, breadth, k6), BF16),
            pltpu.VMEM((count, breadth, k6), BF16),
            pltpu.VMEM((count, breadth, 2 * channels), BF16),
            pltpu.VMEM((count - 1, 2, breadth, channels), F32),
            pltpu.VMEM((2, breadth, channels), F32),
            pltpu.VMEM((4, 2, breadth, channels), BF16),
        ],
        scratch_shapes=[
            pltpu.VMEM((2, height, breadth, channels), BF16),
            pltpu.SemaphoreType.DMA((2, 4)),
        ],
        compiler_params=SMALL,
        cost_estimate=pl.CostEstimate(flops=100000, bytes_accessed=100000, transcendentals=0),
        name="own_column_taps",
    )(*in_hbm(features, upstream), factor)
    row_edges, tx_got = lax.optimization_barrier((row_edges, tx_got))
    ty_sent = pl.pallas_call(
        functools.partial(rows_kernel, kinds_tx),
        in_specs=[VMEM] * (2 + kinds_tx),
        out_specs=[VMEM] * kinds_ty,
        out_shape=[pltpu.VMEM((PLANES, wide, channels), BF16)] * kinds_ty,
        compiler_params=SMALL,
        cost_estimate=pl.CostEstimate(flops=100000000000, bytes_accessed=100000000, transcendentals=0),
        name="edge_rows",
    )(row_edges, factor, *tx_got)
    ty_got = swaps("ty", ty_sent)

    weights = pltpu.VMEM((2, k6, 2 * channels), BF16)
    rows = CHUNK * breadth
    beside_scratch = [
        pltpu.VMEM((8, height + PAST, channels), F32),
        pltpu.VMEM((2, 2 * count, k6), BF16),
        pltpu.VMEM((2, 2 * count, channels), F32),
    ]
    x6, u6, h6, gp2, filters, w_one, w_up, beside_pre = pl.pallas_call(
        functools.partial(middle_kernel, kinds_tx, n_dp),
        in_specs=[VMEM] * (4 + kinds_tx + n_dp),
        out_specs=[VMEM] * 8,
        out_shape=[
            pltpu.VMEM(x6.shape, BF16),
            pltpu.VMEM(u6.shape, BF16),
            pltpu.VMEM((count - 1, breadth, k6), BF16),
            pltpu.VMEM((count, breadth, 2 * channels), BF16),
            pltpu.VMEM((2 * taps, channels, channels), BF16),
            weights,
            weights,
            pltpu.VMEM((2 * count, 2 * channels), F32),
        ],
        input_output_aliases={0: 0, 1: 1},
        scratch_shapes=beside_scratch
        + [
            pltpu.VMEM((count - 1, 2, RIM, channels), F32),
            pltpu.VMEM((4, height, channels), F32),
        ]
        + [pltpu.VMEM((rows, 2 * channels), F32)] * 4,
        compiler_params=pltpu.CompilerParams(vmem_limit_bytes=20 * MIB),
        cost_estimate=pl.CostEstimate(
            flops=2 * 18 * height * breadth * channels * channels,
            bytes_accessed=20 * MIB,
            transcendentals=height * breadth * channels,
        ),
        name="middle_rows",
    )(x6, u6, own_columns, factors, *tx_got, *shards[2:], *shards[:2])

    scale = 1.0 / math.sqrt(height * breadth * n_dp * n_ty * n_tx)
    h6_edges, grad_pre_edges, kept, sent = pl.pallas_call(
        functools.partial(last_kernel, kinds, n_dp, scale),
        in_specs=[VMEM] * (8 + kinds_tx + kinds_ty),
        out_specs=[VMEM] * 4,
        out_shape=[
            pltpu.VMEM((2, breadth, k6), BF16),
            pltpu.VMEM((2, 2, wide, channels), BF16),
            pltpu.VMEM((n_dp // 2, 2 * taps, mine, channels), BF16),
            pltpu.VMEM((n_dp // 2, 2 * taps, mine, channels), BF16),
        ],
        scratch_shapes=[
            pltpu.VMEM((4, wide, k6), BF16),
            pltpu.VMEM((4, wide, k6), BF16),
            pltpu.VMEM((2 * taps, channels, channels), BF16),
        ],
        compiler_params=pltpu.CompilerParams(vmem_limit_bytes=20 * MIB),
        name="outer_rows_and_filter_grads",
    )(x6, row_edges, edge_factors, up2, h6, gp2, w_one, w_up, *tx_got, *ty_got)

    def conv_cost(macs):
        return pl.CostEstimate(
            flops=18 * macs * height * breadth * channels * channels,
            bytes_accessed=4 * height * breadth * channels,
            transcendentals=0,
        )

    def output_step(ready):
        h6_now, _ = lax.optimization_barrier((h6_edges, ready))
        return pl.pallas_call(
            output_kernel,
            in_specs=[VMEM] * 3,
            out_specs=VMEM,
            out_shape=sds(features.shape, BF16),
            scratch_shapes=[weights],
            compiler_params=MEDIUM,
            cost_estimate=conv_cost(1),
            name="output",
        )(h6, h6_now, filters)

    def taps_step(ready):
        edges, _ = lax.optimization_barrier((grad_pre_edges, ready))
        return pl.pallas_call(
            functools.partial(grad_taps_kernel, kinds_tx),
            in_specs=[VMEM] * (6 + kinds_tx),
            out_specs=[VMEM] * 2,
            out_shape=[pltpu.VMEM((pairs, breadth, k6), BF16), weights],
            scratch_shapes=beside_scratch,
            compiler_params=MEDIUM,
            cost_estimate=conv_cost(0),
            name="grad_pre_taps",
        )(gp2, edges, filters, beside_pre, w_up, own_columns, *tx_got)

    def grad_input_step(ready):
        g6, w_back = results.pop()
        g6, _ = lax.optimization_barrier((g6, ready))
        return pl.pallas_call(
            grad_input_kernel,
            in_specs=[VMEM] * 2,
            out_specs=VMEM,
            out_shape=sds(features.shape, BF16),
            compiler_params=MEDIUM,
            cost_estimate=conv_cost(1),
            name="grad_input",
        )(g6, w_back)

    results = []

    def run_between(which, ready, got):
        result = (output_step, taps_step, grad_input_step)[which](ready)
        result, got = lax.optimization_barrier((result, got))
        results.append(result)
        return got

    if (n_dp, n_ty, n_tx) == (4, 4, 2):
        grads = total_by_swaps(kept, sent, run_between)
    else:
        grads = total_by_groups(kept, sent, run_between)
    grads = [g.reshape(3, 3, mine, channels).transpose(0, 1, 3, 2) for g in grads]
    return results[0], results[1], grads[0], grads[1]


def solution(mesh):
    in_specs = (
        P("dp", "ty", "tx", None),
        P(None, None, None, "dp"),
        P(None, None, None, "dp"),
        P("dp", "ty", "tx"),
        P("dp", "ty", "tx"),
        P("dp", None),
        P("dp", "ty", "tx", None),
    )
    out_specs = (
        P("dp", "ty", "tx", None),
        P("dp", "ty", "tx", None),
        P(None, None, None, "dp"),
        P(None, None, None, "dp"),
    )
    return jax.shard_map(
        on_device, mesh=mesh, in_specs=in_specs, out_specs=out_specs, check_vma=False
    )
```

```python
import functools
import math

import jax
import jax.numpy as jnp
from jax import lax
from jax.experimental import pallas as pl
from jax.experimental.pallas import tpu as pltpu
from jax.sharding import PartitionSpec as P

F32 = jnp.float32
BF16 = jnp.bfloat16
RIM = 16
PAST = 8
CHUNK = 16
PLANES = 5
VMEM = pl.BlockSpec(memory_space=pltpu.VMEM)
HBM = pl.BlockSpec(memory_space=pltpu.HBM)
MIB = 1024 * 1024
SMALL = pltpu.CompilerParams(vmem_limit_bytes=8 * MIB)
MEDIUM = pltpu.CompilerParams(vmem_limit_bytes=16 * MIB)


def in_hbm(*arrays):
    return [pltpu.with_memory_space_constraint(array, pltpu.HBM) for array in arrays]


def is_odd(axis):
    return lax.rem(lax.axis_index(axis), 2) == 1


def kind_pairs(count, kind):
    return [(i, i + 1) for i in range(kind, count - 1, 2)]


def swaps(axis, sent):
    got = []
    for kind in reversed(range(len(sent))):
        pairs = [p for i, j in kind_pairs(lax.axis_size(axis), kind) for p in ((i, j), (j, i))]
        got.append(lax.ppermute(sent[kind], axis, pairs))
    return got[::-1]


def sides(axis, got):
    odd = is_odd(axis)
    first = got[0]
    second = got[1] if len(got) > 1 else jnp.zeros_like(first)
    return jnp.where(odd, first, second), jnp.where(odd, second, first)


def rim_of(before, after):
    channels = after[0].shape[1]
    at = lax.broadcasted_iota(jnp.int32, (RIM, channels), 0)
    rim = jnp.where(at == 0, after[0], 0.0)
    if after[1] is not None:
        rim = jnp.where(at == 1, after[1], rim)
    if before[0] is not None:
        rim = jnp.where(at == RIM - 2, before[0], rim)
    return jnp.where(at == RIM - 1, before[1], rim)


def factor_tile(line, channels):
    high = line.astype(BF16).astype(F32)
    low = (line - high).astype(BF16).astype(F32)
    line = jnp.concatenate([high, low, jnp.zeros((RIM - 2, line.shape[1]), F32)])
    past = channels - line.shape[1]
    return line if past == 0 else jnp.concatenate([line, jnp.zeros((RIM, past), F32)], axis=1)


def tx_sides(got, height):
    result = []
    for rows in sides("tx", [ref[...].astype(F32) for ref in got]):
        lines = [rows[n * height : (n + 1) * height] for n in range(4)]
        parts = jnp.transpose(rows[4 * height :])
        result.append((lines, parts[:height, 0:1] + parts[:height, 1:2]))
    return result


def two_parts(column, channels):
    high = column.astype(BF16).astype(F32)
    low = (column - high).astype(BF16).astype(F32)
    lane = lax.broadcasted_iota(jnp.int32, (column.shape[0], channels), 1)
    return jnp.where(lane == 0, high, jnp.where(lane == 1, low, 0.0))


def columns_kernel(kinds_tx, offsets, features, upstream, speedup, land, one, two, *rest):
    sent, rest = rest[:kinds_tx], rest[kinds_tx:]
    factor_ref, filters_ref, own_columns, spread, blocks, speed, mask, place, sems = rest
    _, height, breadth = speedup.shape
    channels = features.shape[3]
    taps = one.shape[0]
    ends = (pl.ds(0, RIM), pl.ds(breadth - RIM, RIM))
    moves = [(speedup, speed), (land, mask), (offsets, place)]
    moves += [
        (ref.at[0, :, ends[side], :], blocks.at[2 * array + side])
        for array, ref in enumerate((features, upstream))
        for side in range(2)
    ]
    moves += [(one, filters_ref.at[pl.ds(0, taps)]), (two, filters_ref.at[pl.ds(taps, taps)])]
    copies = [pltpu.make_async_copy(*move, sems.at[n]) for n, move in enumerate(moves)]
    for copy in copies:
        copy.start()
    for copy in copies[:3]:
        copy.wait()
    shape = (height, breadth)
    row = place[0, 0] + lax.axis_index("ty") * height + lax.broadcasted_iota(jnp.int32, shape, 0)
    col = place[0, 1] + lax.axis_index("tx") * breadth + lax.broadcasted_iota(jnp.int32, shape, 1)
    factor = jnp.where(mask[0] == 1, speed[0], jnp.float32(1.0))
    factor = factor / (1.0 + row.astype(F32) / 512.0) / (1.0 + col.astype(F32) / 1024.0)
    factor_ref[...] = factor
    odd = is_odd("tx")

    def column(at):
        return spread[pl.ds(at, height, stride=RIM), :]

    heads, tails = [], []
    for array in range(2):
        copies[3 + 2 * array].wait()
        spread[: height * RIM] = blocks[2 * array].astype(F32).reshape(height * RIM, channels)
        heads += [column(0), column(1)]
        copies[4 + 2 * array].wait()
        spread[: height * RIM] = blocks[2 * array + 1].astype(F32).reshape(height * RIM, channels)
        tails += [column(RIM - 2), column(RIM - 1)]
    across = jnp.transpose(factor)
    heads.append(factor_tile(across[:1], channels))
    tails.append(factor_tile(across[breadth - 1 :], channels))
    for plane in range(PLANES):
        rows = slice(plane * height, min((plane + 1) * height, sent[0].shape[0]))
        sent[0][rows] = jnp.where(odd, heads[plane], tails[plane]).astype(BF16)
        if kinds_tx == 2:
            sent[1][rows] = jnp.where(odd, tails[plane], heads[plane]).astype(BF16)
    for array in range(2):
        own_columns[2 * array] = heads[2 * array].astype(BF16)
        own_columns[2 * array + 1] = tails[2 * array + 1].astype(BF16)
    for copy in copies[7:]:
        copy.wait()


def rows_kernel(kinds_tx, edges, factor_ref, *rest):
    got, sent = rest[:kinds_tx], rest[kinds_tx:]
    height, breadth = factor_ref.shape
    channels = edges.shape[3]
    across = jnp.transpose(factor_ref[...])
    (before, factor_before), (after, factor_after) = tx_sides(got, height)

    def message(side, lines, edge):
        planes = []
        for array in range(2):
            for n, line in enumerate(lines):
                rim = rim_of(
                    [before[2 * array + i][line : line + 1] for i in range(2)],
                    [after[2 * array + i][line : line + 1] for i in range(2)],
                )
                planes.append(jnp.concatenate([edges[2 * array + side, n].astype(F32), rim]))
        own = two_parts(across[:, edge : edge + 1], channels)
        rim = rim_of(
            (None, two_parts(factor_before[edge : edge + 1], channels)),
            (two_parts(factor_after[edge : edge + 1], channels), None),
        )
        planes.append(jnp.concatenate([own, rim]))
        return planes

    heads = message(0, (0, 1), 0)
    tails = message(1, (height - 2, height - 1), height - 1)
    odd = is_odd("ty")
    for plane in range(PLANES):
        sent[0][plane] = jnp.where(odd, heads[plane], tails[plane]).astype(BF16)
        if len(sent) == 2:
            sent[1][plane] = jnp.where(odd, tails[plane], heads[plane]).astype(BF16)


def pair_weights(target, block_of):
    channels = target.shape[2] // 2
    for half in range(2):
        for s in range(2):
            for t in range(2):
                a = 2 * half + s - t
                for e in range(3):
                    block = block_of(a, e) if 0 <= a <= 2 else jnp.zeros((channels, channels), BF16)
                    at = (3 * s + e) * channels
                    target[half, at : at + channels, t * channels : (t + 1) * channels] = block


def store_taps(target, where, s, wide, width):
    channels = wide.shape[-1]
    axis = wide.ndim - 2
    for e in range(3):
        if e == 1:
            moved = wide
        else:
            moved = pltpu.roll(wide, 1 if e == 0 else wide.shape[axis] - 1, axis)
        moved = moved[..., :width, :].astype(BF16)
        target[where, :, (3 * s + e) * channels : (3 * s + e + 1) * channels] = moved


def pair_conv(source, weights, at, pairs):
    _, width, depth = source.shape
    upper = source[at : at + pairs].reshape(pairs * width, depth)
    lower = source[at + 1 : at + 1 + pairs].reshape(pairs * width, depth)
    return deep_product(upper, lower, weights)


def deep_product(upper, lower, weights):
    _, depth, lanes = weights.shape
    return jnp.dot(
        jnp.concatenate([upper, lower], axis=1),
        weights[...].reshape(2 * depth, lanes),
        preferred_element_type=F32,
    )


def outer(grads, source):
    return lax.dot_general(grads, source, (((0,), (0,)), ((), ())), preferred_element_type=F32)


def own_kernel(
    features, upstream, factor_ref, x6, u6, up2, factors, edge_factors, edges, cells, sems
):
    _, height, breadth, channels = features.shape
    arrays = (features, upstream)
    parts = sems.shape[1]
    rows = height // parts
    copies = [
        [
            pltpu.make_async_copy(
                ref.at[0, pl.ds(n * rows, rows)],
                cells.at[array, pl.ds(n * rows, rows)],
                sems.at[array, n],
            )
            for array, ref in enumerate(arrays)
        ]
        for n in range(parts)
    ]
    for pair in copies:
        for copy in pair:
            copy.start()
    across = jnp.transpose(factor_ref[...])
    for i in range(height):
        line = jnp.broadcast_to(across[:, i : i + 1], (breadth, channels))
        if i in (0, height - 1):
            edge_factors[min(i, 1)] = line
        else:
            factors[(i - 1) // 2, (i - 1) % 2] = line

    def spread(q, carry):
        for s in range(2):
            for array, target in enumerate((x6, u6)):
                line = cells[array, 2 * q + s]
                store_taps(target, q, s, line.astype(F32), breadth)
            up2[q, :, s * channels : (s + 1) * channels] = line
        return carry

    for n, pair in enumerate(copies):
        for copy in pair:
            copy.wait()
        lax.fori_loop(n * rows // 2, (n + 1) * rows // 2, spread, 0)
    for array in range(2):
        edges[2 * array] = cells[array, :2]
        edges[2 * array + 1] = cells[array, height - 2 :]


def activations(pre, grad, factor):
    s = 0.5 * jnp.tanh(0.5 * pre) + 0.5
    fs = factor * s
    return pre * fs, grad * fs * (1.0 + pre * (1.0 - s))


class Beside:
    def __init__(self, array, got_tx, own_columns, columns):
        channels = columns.shape[2]
        height = columns.shape[1] - PAST
        self.array, self.columns, self.count = array, columns, height // 2
        (before, factor_before), (after, factor_after) = tx_sides(got_tx, height)
        own = own_columns[...].astype(F32)
        lines = (
            before[2 * array],
            before[2 * array + 1],
            own[2 * array],
            own[2 * array + 1],
            after[2 * array],
            after[2 * array + 1],
            jnp.broadcast_to(factor_before, (height, channels)),
            jnp.broadcast_to(factor_after, (height, channels)),
        )
        for n, line in enumerate(lines):
            columns[n, :height] = line
        columns[:, height:] = jnp.zeros((len(lines), PAST, channels), F32)

    def rows(self, n, begin):
        return self.columns[n, pl.ds(begin, self.count, stride=2), :]

    def conv(self, taps6, weights):
        count, channels = self.count, self.columns.shape[2]
        for half in range(2):
            for s in range(2):
                for side in range(2):
                    for e in range(3):
                        at = (3 * s + e) * channels
                        taps6[half, side * count : (side + 1) * count, at : at + channels] = (
                            self.rows(3 * side + e, 2 * half + s).astype(BF16)
                        )
        return deep_product(taps6[0], taps6[1], weights)

    def factor(self, t):
        return jnp.concatenate([self.rows(6, 1 + t), self.rows(7, 1 + t)])


def rims_of(lines, begin, pairs, count):
    return [
        [
            rim_of((None, lines[t, m : m + 1, :]), (lines[t, count + m : count + m + 1, :], None))
            for t in range(2)
        ]
        for m in range(begin, begin + pairs)
    ]


def middle_kernel(kinds_tx, n_dp, x6_in, u6_in, own_columns, factors, *rest):
    got_tx, rest = rest[:kinds_tx], rest[kinds_tx:]
    shards, rest = rest[n_dp - 2 : n_dp] + rest[: n_dp - 2], rest[n_dp:]
    x6, u6, h6, gp2, filters_ref, w_one, w_up, beside_pre = rest[:8]
    columns, beside6, beside_hidden, hidden_rims, edge_cells = rest[8:13]
    pres, grads = rest[13:15], rest[15:17]
    count, breadth, _ = x6.shape
    channels = columns.shape[2]
    mine = shards[0].shape[1]
    me = lax.axis_index("dp")
    for partner, shard in enumerate(shards):
        slot = jnp.bitwise_xor(me, partner)
        filters_ref[:, pl.ds(pl.multiple_of(slot * mine, mine), mine), :] = shard[...]
    pair_weights(w_one, lambda a, e: jnp.transpose(filters_ref[3 * a + e]))
    (before, _), (after, _) = tx_sides(got_tx, 2 * count)
    for array in range(2):
        edge_cells[2 * array] = before[2 * array + 1]
        edge_cells[2 * array + 1] = after[2 * array]
    spot = lax.broadcasted_iota(jnp.int32, (RIM, channels), 0)
    first, last = slice(0, RIM), slice(breadth - RIM, breadth)

    def patch(array, begin, end):
        source, target = ((x6_in, x6), (u6_in, u6))[array]
        for q in range(begin, end):
            for s in range(2):
                i = 2 * q + s
                for e, rows, at in ((0, first, 0), (2, last, RIM - 1)):
                    cell = edge_cells[2 * array + e // 2, i : i + 1, :]
                    lanes = slice((3 * s + e) * channels, (3 * s + e + 1) * channels)
                    value = jnp.where(spot == at, cell, source[q, rows, lanes].astype(F32))
                    target[q, rows, lanes] = value.astype(BF16)

    def convolve(n, at, pairs):
        rows = pairs * breadth
        pres[n % 2][:rows] = pair_conv(x6, w_one, at, pairs)
        grads[n % 2][:rows] = pair_conv(u6, w_up, at, pairs)

    def activate(n, at, pairs):
        rows = pairs * breadth
        here = slice(at, at + pairs)
        for t in range(2):
            lanes = slice(t * channels, (t + 1) * channels)
            hidden, grad_pre = activations(
                pres[n % 2][:rows, lanes],
                grads[n % 2][:rows, lanes],
                factors[here, t].reshape(rows, channels),
            )
            hidden = hidden.reshape(pairs, breadth, channels)
            grad_pre = grad_pre.astype(BF16).reshape(pairs, breadth, channels)
            store_taps(
                h6, here, t, jnp.concatenate([hidden, hidden_rims[here, t]], axis=1), breadth
            )
            gp2[at + t : at + t + pairs, :, (1 - t) * channels : (2 - t) * channels] = grad_pre

    chunks = [(0, 0)]
    while sum(chunks[-1]) < count - 1:
        left = count - 1 - sum(chunks[-1])
        chunks.append((sum(chunks[-1]), min(left, CHUNK, max(3, (left + 1) // 2))))
    del chunks[0]
    done = 0
    for n, (at, pairs) in enumerate(chunks):
        for array in range(2):
            patch(array, done, at + pairs + 1)
        done = at + pairs + 1
        if n == 0:
            pair_weights(w_up, lambda a, e: filters_ref[9 + 3 * (2 - a) + (2 - e)])
        convolve(n, at, pairs)
        if n == 0:
            beside = Beside(0, got_tx, own_columns, columns)
            beside_pre[...] = beside.conv(beside6, w_one)
            for t in range(2):
                lanes = slice(t * channels, (t + 1) * channels)
                beside_hidden[t], _ = activations(beside_pre[:, lanes], 0.0, beside.factor(t))
        for m, rims in enumerate(rims_of(beside_hidden, at, pairs, count)):
            for t in range(2):
                hidden_rims[at + m, t] = rims[t]
        if n > 0:
            activate(n - 1, *chunks[n - 1])
    activate(len(chunks) - 1, *chunks[-1])


def last_kernel(kinds, n_dp, scale, x6, row_edges, edge_factors, up2, h6, gp2, w_one, w_up, *rest):
    kinds_ty, kinds_tx = kinds
    got_tx, rest = rest[:kinds_tx], rest[kinds_tx:]
    got_ty, rest = rest[:kinds_ty], rest[kinds_ty:]
    he, grad_pre_ref, keep_ref, send_ref, xe, ue, sums = rest
    count, breadth, _ = x6.shape
    wide, height = breadth + RIM, 2 * count
    channels = edge_factors.shape[2]
    me = lax.axis_index("dp")

    half = 3 * channels
    taps = 9
    c = channels
    near, far = 2, count - 2

    def flat(value):
        return value.reshape(-1, value.shape[-1])

    def joined(*values):
        return jnp.concatenate(values, axis=1)

    two = outer(
        flat(up2[near:far]), joined(flat(h6[near - 1 : far - 1]), flat(h6[near:far]))
    )
    (before, factor_before), (after, factor_after) = tx_sides(got_tx, height)
    got_rows = sides("ty", [ref[...].astype(F32) for ref in got_ty[::-1]])
    lines = []
    for side, planes in enumerate(got_rows):
        for array, target in enumerate((xe, ue)):
            for s in range(2):
                store_taps(target, 3 * side, s, planes[2 * array + s], wide)
                i = s if side == 0 else height - 2 + s
                rim = rim_of(
                    [before[2 * array + n][i : i + 1] for n in range(2)],
                    [after[2 * array + n][i : i + 1] for n in range(2)],
                )
                own = row_edges[2 * array + side, s].astype(F32)
                store_taps(target, 1 + side, s, jnp.concatenate([own, rim]), wide)
        outer_line = jnp.broadcast_to(planes[4][:, 0:1] + planes[4][:, 1:2], (wide, channels))
        i = 0 if side == 0 else height - 1
        ends = [
            jnp.broadcast_to(column[i : i + 1], (1, channels))
            for column in (factor_before, factor_after)
        ]
        rim = rim_of((None, ends[0]), (ends[1], None))
        inner_line = jnp.concatenate([edge_factors[side], rim])
        lines.append((outer_line, inner_line) if side == 0 else (inner_line, outer_line))

    def edge_conv(lines, weights):
        upper = jnp.concatenate([lines[0], lines[2]])
        lower = jnp.concatenate([lines[1], lines[3]])
        return deep_product(upper, lower, weights)

    pre = edge_conv(xe, w_one)
    grad = edge_conv(ue, w_up)
    one = outer(
        flat(gp2[near:far]),
        joined(
            flat(x6[near - 1 : far - 1, :, half:]),
            flat(x6[near:far]),
            flat(x6[near + 1 : far + 1, :, :half]),
        ),
    )
    inner_grads = []
    for side in range(2):
        rows = slice(side * wide, (side + 1) * wide)
        for t in range(2):
            lanes = slice(t * channels, (t + 1) * channels)
            hidden, grad_pre = activations(pre[rows, lanes], grad[rows, lanes], lines[side][t])
            grad_pre_ref[side, t] = grad_pre.astype(BF16)
            store_taps(he, side, t, hidden, breadth)
            if t != side:
                inner_grads.append(grad_pre[:breadth].astype(BF16))

    def ends(*values):
        return jnp.concatenate([flat(value) for value in values])

    two += outer(
        ends(up2[:near], up2[far:]),
        joined(
            ends(he[0], h6[: near - 1], h6[far - 1 :]),
            ends(h6[:near], h6[far:], he[1]),
        ),
    )
    one += outer(
        ends(
            joined(inner_grads[0], gp2[0, :, c:]),
            gp2[1:near],
            gp2[far : count - 1],
            joined(gp2[count - 1, :, :c], inner_grads[1]),
        ),
        joined(
            ends(xe[0, :breadth, half:], x6[: near - 1, :, half:], x6[far - 1 : count - 1, :, half:]),
            ends(x6[:near], x6[far:]),
            ends(x6[1 : near + 1, :, :half], x6[far + 1 :, :, :half], xe[3, :breadth, :half]),
        ),
    )

    def write(level_at, a, total):
        for e in range(3):
            part = (total[:, e * channels : (e + 1) * channels] * scale).astype(BF16)
            sums[level_at * taps + 3 * a + e] = part

    first, second = two[:, : 2 * half], two[:, 2 * half :]
    write(1, 0, first[:c, :half] + first[c:, half:])
    write(1, 1, first[:c, half:] + second[c:, :half])
    write(1, 2, second[:c, :half] + second[c:, half:])
    first, second, third = one[:, :half], one[:, half : 3 * half], one[:, 3 * half :]
    write(0, 0, first[:c] + second[c:, :half])
    write(0, 1, second[:c, :half] + second[c:, half:])
    write(0, 2, second[:c, half:] + third[c:])
    mine = keep_ref.shape[2]
    for partner in range(n_dp):
        slot = jnp.bitwise_xor(me, partner)
        target = send_ref if partner % 2 else keep_ref
        target[partner // 2] = sums[:, pl.ds(pl.multiple_of(slot * mine, mine), mine), :]


def output_kernel(middle, edges, filters, target, weights):
    count, breadth, _ = middle.shape
    channels = target.shape[3]
    pair_weights(weights, lambda a, e: jnp.transpose(filters[9 + 3 * a + e]))

    def write(result, at, pairs):
        for n in range(pairs):
            for t in range(2):
                target[0, 2 * (at + n) + t] = result[
                    n * breadth : (n + 1) * breadth, t * channels : (t + 1) * channels
                ]

    for at in range(0, count - 1, 2 * CHUNK):
        pairs = min(2 * CHUNK, count - 1 - at)
        write(pair_conv(middle, weights, at, pairs).astype(BF16), at + 1, pairs)
    upper = jnp.concatenate([edges[0], middle[count - 1]])
    lower = jnp.concatenate([middle[0], edges[1]])
    result = deep_product(upper, lower, weights)
    write(result[:breadth].astype(BF16), 0, 1)
    write(result[breadth:].astype(BF16), count, 1)


def grad_taps_kernel(kinds_tx, gp2, edges, filters, beside_pre, w_up, own_columns, *rest):
    got_tx, rest = rest[:kinds_tx], rest[kinds_tx:]
    taps6, weights, columns, beside6, beside_grad = rest
    pairs, breadth, _ = taps6.shape
    channels = columns.shape[2]
    pair_weights(weights, lambda a, e: filters[3 * (2 - a) + (2 - e)])
    beside = Beside(1, got_tx, own_columns, columns)
    grad = beside.conv(beside6, w_up)
    for t in range(2):
        lanes = slice(t * channels, (t + 1) * channels)
        _, beside_grad[t] = activations(beside_pre[:, lanes], grad[:, lanes], beside.factor(t))
    rims = rims_of(beside_grad, 0, pairs - 2, pairs - 1)
    for q in range(pairs - 2):
        for s in range(2):
            line = gp2[q + s, :, (1 - s) * channels : (2 - s) * channels].astype(F32)
            store_taps(taps6, q + 1, s, jnp.concatenate([line, rims[q][s]]), breadth)
    for side, q in enumerate((0, pairs - 1)):
        for s in range(2):
            store_taps(taps6, q, s, edges[side, s].astype(F32), breadth)


def grad_input_kernel(taps6, weights, target):
    pairs, breadth, _ = taps6.shape
    channels = target.shape[3]
    for at in range(0, pairs - 1, 2 * CHUNK):
        many = min(2 * CHUNK, pairs - 1 - at)
        result = pair_conv(taps6, weights, at, many).astype(BF16)
        for n in range(many):
            for t in range(2):
                target[0, 2 * (at + n) + t] = result[
                    n * breadth : (n + 1) * breadth, t * channels : (t + 1) * channels
                ]


def split_kernel(kept, got, own, *others):
    near = lax.axis_index("tx")
    far = 1 - near
    taps = own.shape[0]
    for target, half, at in zip((own,) + others, (near, near, far, far), (0, 1, 0, 1)):
        rows = pl.ds(half * taps, taps)
        target[...] = (kept[at, rows].astype(F32) + got[at, rows].astype(F32)).astype(BF16)


def total_kernel(*refs):
    total = refs[0][...].astype(F32)
    for ref in refs[1:-1]:
        total += ref[...].astype(F32)
    refs[-1][...] = total.astype(BF16)


def halves_kernel(own, by_both, by_x, by_y, one, two):
    first = lax.axis_index("tx") == 0
    near = own[...].astype(F32) + by_y[...].astype(F32)
    far = by_x[...].astype(F32) + by_both[...].astype(F32)
    one[...] = jnp.where(first, near, far)
    two[...] = jnp.where(first, far, near)


def add_kernel(more, kept, got, keep_ref, send_ref):
    for n in range(kept.shape[0]):
        total = (kept[n].astype(F32) + got[n].astype(F32)).astype(BF16)
        if more and n % 2:
            send_ref[n // 2] = total
        else:
            keep_ref[n // 2] = total


def sum_kernel(got, total_ref):
    total = got[0].astype(F32)
    for source in range(1, got.shape[0]):
        total += got[source].astype(F32)
    for copy in range(total_ref.shape[0]):
        total_ref[copy] = total.astype(BF16)


def partners(axis, bit):
    return [(i, i ^ bit) for i in range(lax.axis_size(axis))]


def total_by_swaps(kept, sent, run_between):
    sds = jax.ShapeDtypeStruct
    _, taps, mine, channels = kept.shape
    piece = sds((taps // 2, mine, channels), BF16)

    def total(*pieces):
        return pl.pallas_call(
            total_kernel,
            in_specs=[VMEM] * len(pieces),
            out_specs=VMEM,
            out_shape=piece,
            compiler_params=SMALL,
            name="sum_of_pieces",
        )(*pieces)

    got = lax.ppermute(sent, "dp", partners("dp", 1))
    own, by_y, by_x, by_both = pl.pallas_call(
        split_kernel,
        in_specs=[VMEM] * 2,
        out_specs=[VMEM] * 4,
        out_shape=[piece] * 4,
        compiler_params=SMALL,
        name="sum_on_chip",
    )(kept, got)
    both = [(2 * i + j, 2 * (i ^ 2) + (j ^ 1)) for i in range(4) for j in range(2)]
    got = [
        lax.ppermute(by_both, ("dp", "tx"), both),
        lax.ppermute(by_y, "dp", partners("dp", 2)),
        lax.ppermute(by_x, "tx", partners("tx", 1)),
    ]
    got = run_between(0, own, got)
    own = total(own, *got)
    got = run_between(1, own, [lax.ppermute(own, "ty", partners("ty", 2))])
    own = total(own, *got)
    both = [(2 * i + j, 2 * (i ^ 1) + (j ^ 1)) for i in range(4) for j in range(2)]
    got = [
        lax.ppermute(own, ("ty", "tx"), both),
        lax.ppermute(own, "tx", partners("tx", 1)),
        lax.ppermute(own, "ty", partners("ty", 1)),
    ]
    return pl.pallas_call(
        halves_kernel,
        in_specs=[VMEM] * 4,
        out_specs=[VMEM] * 2,
        out_shape=[sds(piece.shape, F32)] * 2,
        compiler_params=SMALL,
        name="both_halves",
    )(own, *got)


def total_by_groups(kept, sent, run_between):
    sds = jax.ShapeDtypeStruct
    _, taps, mine, channels = kept.shape
    n_dp = lax.axis_size("dp")
    bit = 1
    while bit < n_dp:
        got = lax.ppermute(sent, "dp", partners("dp", bit))
        half = kept.shape[0] // 2
        bit *= 2
        kept, sent = pl.pallas_call(
            functools.partial(add_kernel, bit < n_dp),
            in_specs=[VMEM] * 2,
            out_specs=[VMEM] * 2,
            out_shape=[sds((max(half, 1),) + kept.shape[1:], BF16)] * 2,
            compiler_params=SMALL,
            name="sum_of_crops",
        )(kept, got)
    tiles = lax.axis_size("ty") * lax.axis_size("tx")
    rows = taps * mine // tiles
    got = lax.all_to_all(kept.reshape(tiles, rows, channels), ("ty", "tx"), 0, 0, tiled=True)
    shared = pl.pallas_call(
        sum_kernel,
        in_specs=[VMEM],
        out_specs=VMEM,
        out_shape=sds((tiles, rows, channels), BF16),
        compiler_params=SMALL,
        name="sum_of_tiles",
    )(got)
    (total,) = run_between(0, shared, [lax.all_to_all(shared, ("ty", "tx"), 0, 0, tiled=True)])
    run_between(1, shared, [total])
    total = total.astype(F32).reshape(2, taps // 2, mine, channels)
    return total[0], total[1]


def on_device(features, filter_one, filter_two, speedup, land_mask, offsets, upstream):
    _, height, breadth, channels = features.shape
    mine = filter_one.shape[3]
    n_dp, n_ty, n_tx = (lax.axis_size(axis) for axis in ("dp", "ty", "tx"))
    kinds = kinds_ty, kinds_tx = min(2, n_ty - 1), min(2, n_tx - 1)
    taps = 9
    wide = breadth + RIM
    pairs = height // 2 + 1
    sds = jax.ShapeDtypeStruct

    one, two = (f.reshape(taps, channels, mine).transpose(0, 2, 1) for f in (filter_one, filter_two))
    *tx_sent, factor, shard, own_columns = pl.pallas_call(
        functools.partial(columns_kernel, kinds_tx),
        in_specs=[HBM] * 7,
        out_specs=[VMEM] * (kinds_tx + 3),
        out_shape=[pltpu.VMEM((4 * height + RIM, channels), BF16)] * kinds_tx
        + [pltpu.VMEM((height, breadth), F32), pltpu.VMEM((2 * taps, mine, channels), BF16)]
        + [pltpu.VMEM((4, height, channels), BF16)],
        scratch_shapes=[
            pltpu.VMEM(((height + 1) * RIM, channels), F32),
            pltpu.VMEM((4, height, RIM, channels), BF16),
            pltpu.VMEM(speedup.shape, F32),
            pltpu.VMEM(land_mask.shape, jnp.int32),
            pltpu.SMEM(offsets.shape, jnp.int32),
            pltpu.SemaphoreType.DMA((9,)),
        ],
        compiler_params=SMALL,
        name="edge_columns",
    )(*in_hbm(offsets, features, upstream, speedup, land_mask, one, two))
    tx_got = swaps("tx", tx_sent)
    shards = [shard] + [
        lax.ppermute(shard, "dp", partners("dp", partner)) for partner in range(1, n_dp)
    ]

    count = height // 2
    k6 = 6 * channels
    x6, u6, up2, factors, edge_factors, row_edges = pl.pallas_call(
        own_kernel,
        in_specs=[HBM] * 2 + [VMEM],
        out_specs=[VMEM] * 6,
        out_shape=[
            pltpu.VMEM((count, breadth, k6), BF16),
            pltpu.VMEM((count, breadth, k6), BF16),
            pltpu.VMEM((count, breadth, 2 * channels), BF16),
            pltpu.VMEM((count - 1, 2, breadth, channels), F32),
            pltpu.VMEM((2, breadth, channels), F32),
            pltpu.VMEM((4, 2, breadth, channels), BF16),
        ],
        scratch_shapes=[
            pltpu.VMEM((2, height, breadth, channels), BF16),
            pltpu.SemaphoreType.DMA((2, 4)),
        ],
        compiler_params=SMALL,
        cost_estimate=pl.CostEstimate(flops=100000, bytes_accessed=100000, transcendentals=0),
        name="own_column_taps",
    )(*in_hbm(features, upstream), factor)
    row_edges, tx_got = lax.optimization_barrier((row_edges, tx_got))
    ty_sent = pl.pallas_call(
        functools.partial(rows_kernel, kinds_tx),
        in_specs=[VMEM] * (2 + kinds_tx),
        out_specs=[VMEM] * kinds_ty,
        out_shape=[pltpu.VMEM((PLANES, wide, channels), BF16)] * kinds_ty,
        compiler_params=SMALL,
        cost_estimate=pl.CostEstimate(flops=100000000000, bytes_accessed=100000000, transcendentals=0),
        name="edge_rows",
    )(row_edges, factor, *tx_got)
    ty_got = swaps("ty", ty_sent)

    weights = pltpu.VMEM((2, k6, 2 * channels), BF16)
    rows = CHUNK * breadth
    beside_scratch = [
        pltpu.VMEM((8, height + PAST, channels), F32),
        pltpu.VMEM((2, 2 * count, k6), BF16),
        pltpu.VMEM((2, 2 * count, channels), F32),
    ]
    x6, u6, h6, gp2, filters, w_one, w_up, beside_pre = pl.pallas_call(
        functools.partial(middle_kernel, kinds_tx, n_dp),
        in_specs=[VMEM] * (4 + kinds_tx + n_dp),
        out_specs=[VMEM] * 8,
        out_shape=[
            pltpu.VMEM(x6.shape, BF16),
            pltpu.VMEM(u6.shape, BF16),
            pltpu.VMEM((count - 1, breadth, k6), BF16),
            pltpu.VMEM((count, breadth, 2 * channels), BF16),
            pltpu.VMEM((2 * taps, channels, channels), BF16),
            weights,
            weights,
            pltpu.VMEM((2 * count, 2 * channels), F32),
        ],
        input_output_aliases={0: 0, 1: 1},
        scratch_shapes=beside_scratch
        + [
            pltpu.VMEM((count - 1, 2, RIM, channels), F32),
            pltpu.VMEM((4, height, channels), F32),
        ]
        + [pltpu.VMEM((rows, 2 * channels), F32)] * 4,
        compiler_params=pltpu.CompilerParams(vmem_limit_bytes=20 * MIB),
        cost_estimate=pl.CostEstimate(
            flops=2 * 18 * height * breadth * channels * channels,
            bytes_accessed=20 * MIB,
            transcendentals=height * breadth * channels,
        ),
        name="middle_rows",
    )(x6, u6, own_columns, factors, *tx_got, *shards[2:], *shards[:2])

    scale = 1.0 / math.sqrt(height * breadth * n_dp * n_ty * n_tx)
    h6_edges, grad_pre_edges, kept, sent = pl.pallas_call(
        functools.partial(last_kernel, kinds, n_dp, scale),
        in_specs=[VMEM] * (8 + kinds_tx + kinds_ty),
        out_specs=[VMEM] * 4,
        out_shape=[
            pltpu.VMEM((2, breadth, k6), BF16),
            pltpu.VMEM((2, 2, wide, channels), BF16),
            pltpu.VMEM((n_dp // 2, 2 * taps, mine, channels), BF16),
            pltpu.VMEM((n_dp // 2, 2 * taps, mine, channels), BF16),
        ],
        scratch_shapes=[
            pltpu.VMEM((4, wide, k6), BF16),
            pltpu.VMEM((4, wide, k6), BF16),
            pltpu.VMEM((2 * taps, channels, channels), BF16),
        ],
        compiler_params=pltpu.CompilerParams(vmem_limit_bytes=20 * MIB),
        name="outer_rows_and_filter_grads",
    )(x6, row_edges, edge_factors, up2, h6, gp2, w_one, w_up, *tx_got, *ty_got[::-1])

    def conv_cost(macs):
        return pl.CostEstimate(
            flops=18 * macs * height * breadth * channels * channels,
            bytes_accessed=4 * height * breadth * channels,
            transcendentals=0,
        )

    def output_step(ready):
        h6_now, _ = lax.optimization_barrier((h6_edges, ready))
        return pl.pallas_call(
            output_kernel,
            in_specs=[VMEM] * 3,
            out_specs=VMEM,
            out_shape=sds(features.shape, BF16),
            scratch_shapes=[weights],
            compiler_params=MEDIUM,
            cost_estimate=conv_cost(1),
            name="output",
        )(h6, h6_now, filters)

    def taps_step(ready):
        edges, _ = lax.optimization_barrier((grad_pre_edges, ready))
        return pl.pallas_call(
            functools.partial(grad_taps_kernel, kinds_tx),
            in_specs=[VMEM] * (6 + kinds_tx),
            out_specs=[VMEM] * 2,
            out_shape=[pltpu.VMEM((pairs, breadth, k6), BF16), weights],
            scratch_shapes=beside_scratch,
            compiler_params=MEDIUM,
            cost_estimate=conv_cost(0),
            name="grad_pre_taps",
        )(gp2, edges, filters, beside_pre, w_up, own_columns, *tx_got)

    def grad_input_step(ready):
        g6, w_back = results.pop()
        g6, _ = lax.optimization_barrier((g6, ready))
        return pl.pallas_call(
            grad_input_kernel,
            in_specs=[VMEM] * 2,
            out_specs=VMEM,
            out_shape=sds(features.shape, BF16),
            compiler_params=MEDIUM,
            cost_estimate=conv_cost(1),
            name="grad_input",
        )(g6, w_back)

    results = []

    def run_between(which, ready, got):
        if which == 0:
            result = output_step(ready)
        else:
            results.append(taps_step(ready))
            result = grad_input_step(ready)
        result, got = lax.optimization_barrier((result, got))
        results.append(result)
        return got

    if (n_dp, n_ty, n_tx) == (4, 4, 2):
        grads = total_by_swaps(kept, sent, run_between)
    else:
        grads = total_by_groups(kept, sent, run_between)
    grads = [g.reshape(3, 3, mine, channels).transpose(0, 1, 3, 2) for g in grads]
    return results[0], results[1], grads[0], grads[1]


def solution(mesh):
    in_specs = (
        P("dp", "ty", "tx", None),
        P(None, None, None, "dp"),
        P(None, None, None, "dp"),
        P("dp", "ty", "tx"),
        P("dp", "ty", "tx"),
        P("dp", None),
        P("dp", "ty", "tx", None),
    )
    out_specs = (
        P("dp", "ty", "tx", None),
        P("dp", "ty", "tx", None),
        P(None, None, None, "dp"),
        P(None, None, None, "dp"),
    )
    return jax.shard_map(
        on_device, mesh=mesh, in_specs=in_specs, out_specs=out_specs, check_vma=False
    )
```
